32 devices in a mesh: groups: 2 (over y), date: 4 (over z), tile: 4 (over x, core).
Axes of the slice: x: 2, y: 2, z: 4, core: 2. Of those that a mesh axis runs over, the one named last changes fastest.
Arguments:
- slc: float32 [24, 2, 128, 1024], P('date', None, 'groups', 'tile'), parts along dimension 2, may hold values from -4 to 4, as said below
- pairs: int32 [64, 2], replicated, may hold values from 0 to 23, as said below
Outputs:
- interferogram: float32 [2, 64, 64, 256], P(None, 'date', 'groups', 'tile'), parts along dimension 2
- coherence: float32 [64, 64, 256], P('date', 'groups', 'tile'), parts along dimension 1
The draws below stay inside these ranges and needn't reach their ends.
There are 2 independent parts, one for each index of `groups`. The reference program is written for one: setup_inputs(seed, part) draws one part's arguments, and reference() takes and returns one part's arrays. A program takes and returns all parts, laid end to end along the dimension named above; an argument that names none is the same for every part. Nothing has to cross between parts.
Inputs may be any that keep to these rules, and one draw needn't show every extreme that they name: Every pair's first date is below its second. In each block of 16 rows (rows k * 16 to (k + 1) * 16 - 1), the distinct dates used that lie among the 6 dates j * 6 to (j + 1) * 6 - 1 number at most 2, for every j; this bound is reached in every block. How many pairs a date takes part in varies. `slc`: every pixel's modulus is at least 0.3.
All inputs are finite; a program needn't handle non-finite values.
Results may differ from the reference program's by a relative error of at most 0.000058.
Values sent between devices are 32-bit elements; how exact they have to be, the bound alone decides.
A program may use at most 128 MiB of HBM per device.

```python
import math
from functools import partial
import jax
import jax.numpy as jnp
from jax import lax

DATE_DEV = 6
NDATES = 24
PAIRS_DEV = 16
NPAIRS = 64
REQ = 2
AZ = 2
RG = 4
PATCH = 32
ROWS = 64
COLS = 1024
LCOLS = 256


def draw_slc(key, part):
    key = jax.random.fold_in(key, 11)
    keys = jax.random.split(key, 6)
    lowest = math.log(0.3)
    highest = math.log(3.0)
    exponent = jax.random.uniform(keys[0], (NDATES, ROWS, COLS), jnp.float32, lowest, highest)
    modulus = jnp.exp(exponent)
    common = jax.random.uniform(keys[1], (1, ROWS, COLS), jnp.float32, -math.pi, math.pi)
    noise_scale = jax.random.uniform(keys[2], (NDATES, 1, 1), jnp.float32, 0.2, 1.2)
    noise = jax.random.normal(keys[3], (NDATES, ROWS, COLS), jnp.float32)
    freq_cols = jax.random.randint(keys[4], (NDATES, 1, 1), 0, 96)
    freq_rows = jax.random.randint(keys[5], (NDATES, 1, 1), 0, 64)
    row_ids = jnp.arange(ROWS, dtype=jnp.int32)[None, :, None] + part * ROWS
    col_ids = jnp.arange(COLS, dtype=jnp.int32)[None, None, :]
    turns = (freq_cols * col_ids + freq_rows * row_ids) % 4096
    phase = common + 2.0 * math.pi / 4096.0 * turns.astype(jnp.float32) + noise_scale * noise
    return jnp.stack([modulus * jnp.cos(phase), modulus * jnp.sin(phase)], axis=1)


def draw_pairs(key, part):
    key = jax.random.fold_in(key, 23)
    keys = jax.random.split(key, 4)
    owners = NPAIRS // PAIRS_DEV
    counts = jax.random.randint(keys[0], (owners, owners), 0, REQ + 1)
    forced = jax.random.randint(keys[1], (owners,), 0, owners)
    sources = jnp.arange(owners, dtype=jnp.int32)
    counts = jnp.where(sources[None, :] == forced[:, None], REQ, counts)
    scores = jax.random.randint(keys[2], (owners, owners, DATE_DEV), 0, 1 << 20)
    inside = jnp.arange(DATE_DEV, dtype=jnp.int32)
    scores = scores * DATE_DEV + inside
    ordering = jnp.argsort(scores, axis=2)
    position = jnp.argsort(ordering, axis=2)
    wanted = (position < counts[:, :, None]).reshape(owners, NDATES)
    dates = jnp.arange(NDATES, dtype=jnp.int32)
    from_forced = dates[None, :] // DATE_DEV == forced[:, None]
    sort_key = jnp.where(wanted, jnp.where(from_forced, dates[None, :], NDATES + dates[None, :]), 2 * NDATES + dates[None, :])
    listing = jnp.argsort(sort_key, axis=1).astype(jnp.int32)
    total = jnp.sum(wanted.astype(jnp.int32), axis=1)
    column = jnp.arange(PAIRS_DEV, dtype=jnp.int32)[None, :]
    offsets = jax.random.randint(keys[3], (owners, PAIRS_DEV), 1, total[:, None])
    first = jnp.take_along_axis(listing, column % total[:, None], axis=1)
    second = jnp.take_along_axis(listing, (column + offsets) % total[:, None], axis=1)
    lower = jnp.minimum(first, second)
    upper = jnp.maximum(first, second)
    return jnp.stack([lower, upper], axis=2).reshape(NPAIRS, 2)


def setup_inputs(seed: int = 0, part: int = 0) -> dict:
    splits = jax.random.split(jax.random.key(seed), 3)
    own_keys = jax.random.split(jax.random.fold_in(splits[2], part), 3)
    slc = draw_slc(jax.random.fold_in(jax.random.fold_in(splits[2], part), 71), part)
    pairs = draw_pairs(jax.random.fold_in(splits[2], 71), part)
    return dict(slc=slc, pairs=pairs)


def look_mean(field):
    return field.reshape(PATCH, AZ, LCOLS, RG).mean(axis=(1, 3))


def goldstein(looked_real, looked_imag):
    half = PATCH // 2
    count = LCOLS // half + 1
    field = lax.complex(looked_real, looked_imag)
    padded = jnp.pad(field, ((0, 0), (half, half)))
    halves = padded.reshape(PATCH, count + 1, half)
    patches = jnp.concatenate([halves[:, :-1], halves[:, 1:]], axis=2)
    patches = jnp.transpose(patches, (1, 0, 2))
    spectrum = jnp.fft.fft2(patches, axes=(1, 2))
    power = jnp.real(spectrum) ** 2 + jnp.imag(spectrum) ** 2
    smooth = jnp.zeros_like(power)
    for row_step in (-1, 0, 1):
        for col_step in (-1, 0, 1):
            smooth = smooth + jnp.roll(power, (row_step, col_step), axis=(1, 2))
    smooth = smooth / 9.0
    level = jnp.mean(smooth, axis=(1, 2), keepdims=True)
    response = ((smooth + 0.1 * level) / (level + 1e-6)) ** 0.25
    filtered = jnp.fft.ifft2(spectrum * response, axes=(1, 2))
    column = jnp.arange(PATCH, dtype=jnp.float32)
    weight = jnp.sin(math.pi * (column + 0.5) / PATCH) ** 2
    filtered = filtered * weight
    summed = filtered[:-1, :, half:] + filtered[1:, :, :half]
    summed = jnp.transpose(summed, (1, 0, 2)).reshape(PATCH, LCOLS)
    return jnp.real(summed), jnp.imag(summed)


def one_pair(slc, pair):
    first = lax.dynamic_index_in_dim(slc, pair[0], 0, keepdims=False)
    second = lax.dynamic_index_in_dim(slc, pair[1], 0, keepdims=False)
    real_prod = first[0] * second[0] + first[1] * second[1]
    imag_prod = first[1] * second[0] - first[0] * second[1]
    power_ref = look_mean(first[0] * first[0] + first[1] * first[1])
    power_sec = look_mean(second[0] * second[0] + second[1] * second[1])
    looked_real = look_mean(real_prod)
    looked_imag = look_mean(imag_prod)
    coherence = (looked_real * looked_real + looked_imag * looked_imag) / (power_ref * power_sec)
    out_real, out_imag = goldstein(looked_real, looked_imag)
    return out_real, out_imag, coherence


def reference(slc, pairs):
    out_real, out_imag, coherence = lax.map(partial(one_pair, slc), pairs)
    return jnp.stack([out_real, out_imag], axis=0), coherence
```

```python
import functools
import math

import jax
import jax.numpy as jnp
import ml_dtypes
import numpy as np
from jax import lax
from jax.experimental import pallas as pl
from jax.experimental.pallas import tpu as pltpu
from jax.sharding import PartitionSpec as P

REQ = 2
AZ = 2
RG = 4
PATCH = 32
HALF = PATCH // 2
GROUP = 4
LANES = 128
MESH = pl.DeviceIdType.MESH
F32 = jnp.float32
BF16 = jnp.bfloat16


def split(value):
    high = value.astype(BF16)
    low = (value - high.astype(F32)).astype(BF16)
    return high, low


def dot(a, b):
    return jnp.dot(a, b, preferred_element_type=F32)


def dot_nt(a, b):
    return lax.dot_general(a, b, (((1,), (1,)), ((), ())), preferred_element_type=F32)


def np_split(table):
    high = table.astype(np.float32).astype(ml_dtypes.bfloat16)
    low = (table - high.astype(np.float64)).astype(np.float32).astype(ml_dtypes.bfloat16)
    return high, low


def look_table(cols):
    looked = cols // RG
    hit = np.arange(cols)[None, :] // RG == np.arange(looked)[:, None]
    return (hit / (AZ * RG)).astype(np.float32).astype(ml_dtypes.bfloat16)


def blocks(small):
    size = small.shape[0] * small.shape[1]
    small = small.reshape(size, size)
    return np.kron(np.eye(GROUP), small)


def filter_tables(looked):
    count = looked // HALF + 1
    index = np.arange(PATCH)
    angle = 2.0 * math.pi / PATCH * ((index[:, None] * index[None, :]) % PATCH)
    cos, sin = np.cos(angle), np.sin(angle)
    wide = looked + PATCH
    fwd_cos = np.zeros((count * PATCH, wide))
    fwd_sin = np.zeros((count * PATCH, wide))
    inv_cos = np.zeros((looked, count * PATCH))
    inv_sin = np.zeros((looked, count * PATCH))
    weight = np.sin(math.pi * (index + 0.5) / PATCH) ** 2 / (PATCH * PATCH)
    for k in range(count):
        rows = slice(k * PATCH, (k + 1) * PATCH)
        fwd_cos[rows, k * HALF : k * HALF + PATCH] = cos
        fwd_sin[rows, k * HALF : k * HALF + PATCH] = sin
        for u in range(PATCH):
            t = u - HALF + k * HALF
            if 0 <= t < looked:
                inv_cos[t, rows] = weight[u] * cos[u]
                inv_sin[t, rows] = weight[u] * sin[u]
    fwd_col = np.concatenate([fwd_cos, fwd_sin], axis=0)
    inv_col = np.concatenate([inv_cos, inv_sin], axis=1)

    def pair_block(rr, ri, ir, ii):
        small = np.zeros((2, PATCH, 2, PATCH))
        small[0, :, 0], small[0, :, 1], small[1, :, 0], small[1, :, 1] = rr, ri, ir, ii
        return blocks(small)

    fwd_row = np.concatenate(
        [pair_block(cos, -sin, sin, cos), pair_block(-sin, -cos, cos, -sin)], axis=0
    )
    inv_row = np.concatenate(
        [pair_block(cos, sin, -sin, cos), pair_block(-sin, cos, -cos, -sin)], axis=1
    )
    apart = (index[:, None] - index[None, :]) % PATCH
    box = ((apart == 0) | (apart == 1) | (apart == PATCH - 1)).astype(np.float64)
    ones = np.ones((PATCH, PATCH))
    zero = np.zeros((PATCH, PATCH))
    box_row = pair_block(box, box, box, box).astype(np.float32).astype(ml_dtypes.bfloat16)
    sum_row = pair_block(ones, zero, zero, ones).astype(np.float32).astype(ml_dtypes.bfloat16)
    return (
        *np_split(fwd_col),
        *np_split(fwd_row),
        box_row,
        sum_row,
        *np_split(inv_row),
        *np_split(inv_col),
    )


def gather_kernel(
    owners, tiles, pair_count,
    pairs_ref, slc_ref, look_ref, look_t_ref, wide_ref, coh_ref,
    send, recv, low_tab, prods, powers, natural, power_looked, looked, halo_low, halo_high,
    send_sem, recv_sem, halo_send_sem, halo_recv_sem,
):
    me = lax.axis_index("date")
    tile = lax.axis_index("tile")
    dates_here = slc_ref.shape[0]
    half_rows = slc_ref.shape[2] // AZ
    cols = slc_ref.shape[3]
    local_cols = cols // RG

    barrier = pltpu.get_barrier_semaphore()
    for offset in range(1, owners):
        pl.semaphore_signal(
            barrier, inc=1, device_id={"date": lax.rem(me + offset, owners)}, device_id_type=MESH
        )

    @pl.when(tile > 0)
    def _():
        pl.semaphore_signal(barrier, inc=1, device_id={"tile": tile - 1}, device_id_type=MESH)

    @pl.when(tile < tiles - 1)
    def _():
        pl.semaphore_signal(barrier, inc=1, device_id={"tile": tile + 1}, device_id_type=MESH)

    def ends(block, source):
        first = source * dates_here

        def step(i, carry):
            low, high = carry
            for c in range(2):
                date = pairs_ref[block * pair_count + i, c] - first
                inside = (date >= 0) & (date < dates_here)
                low = jnp.where(inside, jnp.minimum(low, date), low)
                high = jnp.where(inside, jnp.maximum(high, date), high)
            return low, high

        low, high = lax.fori_loop(
            0, pair_count, step, (jnp.int32(dates_here - 1), jnp.int32(0)), unroll=True
        )
        return low, high

    def stage(target, low, high):
        for rank, pick in ((0, low), (1, high)):
            for part in range(2):
                for lane in range(cols // LANES):
                    target[rank, part, lane] = slc_ref[
                        pick, part, :, lane * LANES : (lane + 1) * LANES
                    ]

    def date_copy(offset, source, target):
        return pltpu.make_async_remote_copy(
            src_ref=send.at[offset - 1],
            dst_ref=recv.at[source],
            send_sem=send_sem.at[offset - 1],
            recv_sem=recv_sem.at[source],
            device_id={"date": target},
            device_id_type=MESH,
        )

    for offset in range(1, owners):
        target = lax.rem(me + offset, owners)
        low, high = ends(target, me)
        stage(send.at[offset - 1], low, high)
        if offset == 1:
            below = lax.div(tile + tiles - 1, tiles)
            above = lax.div(2 * (tiles - 1) - tile, tiles)
            pl.semaphore_wait(barrier, owners - 1 + below + above)

        date_copy(offset, me, target).start()

    low, high = ends(me, me)
    stage(recv.at[me], low, high)
    for source in range(owners):
        low, _ = ends(me, jnp.int32(source))
        low_tab[source] = low + source * dates_here

    for offset in range(1, owners):
        source = lax.rem(me + owners - offset, owners)
        date_copy(offset, source, source).wait_recv()

    def slot(i, c):
        date = pairs_ref[me * pair_count + i, c]
        source = lax.div(date, jnp.int32(dates_here))
        rank = jnp.where(date == low_tab[source], 0, 1)
        return source, rank

    def product(i, _):
        sa, ra = slot(i, 0)
        sb, rb = slot(i, 1)
        for lane in range(cols // LANES):
            real = jnp.zeros((half_rows, LANES), F32)
            imag = jnp.zeros((half_rows, LANES), F32)
            for odd in range(AZ):
                rows = pl.ds(odd, half_rows, stride=AZ)
                a0, a1 = recv[sa, ra, 0, lane, rows, :], recv[sa, ra, 1, lane, rows, :]
                b0, b1 = recv[sb, rb, 0, lane, rows, :], recv[sb, rb, 1, lane, rows, :]
                real = real + (a0 * b0 + a1 * b1)
                imag = imag + (a1 * b0 - a0 * b1)
            prods[i, 0, :, lane * LANES : (lane + 1) * LANES] = real
            prods[i, 1, :, lane * LANES : (lane + 1) * LANES] = imag
        return 0

    lax.fori_loop(0, pair_count, product, 0)
    high, low = split(prods[...].reshape(pair_count * 2 * half_rows, cols))
    table = look_ref[...]
    looked[...] = dot_nt(table, high) + dot_nt(table, low)

    def halo_copy(up):
        step = 1 if up else -1
        return pltpu.make_async_remote_copy(
            src_ref=looked.at[pl.ds(local_cols - HALF if up else 0, HALF)],
            dst_ref=halo_low if up else halo_high,
            send_sem=halo_send_sem.at[0 if up else 1],
            recv_sem=halo_recv_sem.at[0 if up else 1],
            device_id={"tile": tile + step},
            device_id_type=MESH,
        )

    @pl.when(tile < tiles - 1)
    def _():
        halo_copy(True).start()

    @pl.when(tile > 0)
    def _():
        halo_copy(False).start()

    table_t = look_t_ref[...]
    natural[...] = (dot(high, table_t) + dot(low, table_t)).reshape(natural.shape)

    def power(i, _):
        for rank in range(REQ):
            for lane in range(cols // LANES):
                total = jnp.zeros((half_rows, LANES), F32)
                for part in range(2):
                    for odd in range(AZ):
                        field = recv[i, rank, part, lane, pl.ds(odd, half_rows, stride=AZ), :]
                        total = total + field * field
                powers[i, rank, :, lane * LANES : (lane + 1) * LANES] = total
        return 0

    lax.fori_loop(0, owners, power, 0)
    high, low = split(powers[...].reshape(owners * REQ * half_rows, cols))
    power_looked[...] = (dot(high, table_t) + dot(low, table_t)).reshape(power_looked.shape)

    def coherence(i, _):
        sa, ra = slot(i, 0)
        sb, rb = slot(i, 1)
        real, imag = natural[i, 0], natural[i, 1]
        coh_ref[i] = (real * real + imag * imag) / (power_looked[sa, ra] * power_looked[sb, rb])
        return 0

    lax.fori_loop(0, pair_count, coherence, 0)
    wide_ref[pl.ds(HALF, local_cols)] = looked[...]

    @pl.when(tile > 0)
    def _():
        halo_copy(True).wait_recv()
        wide_ref[pl.ds(0, HALF)] = halo_low[...]

    @pl.when(tile == 0)
    def _():
        wide_ref[pl.ds(0, HALF)] = jnp.zeros(halo_low.shape, F32)

    @pl.when(tile < tiles - 1)
    def _():
        halo_copy(False).wait_recv()
        wide_ref[pl.ds(HALF + local_cols, HALF)] = halo_high[...]

    @pl.when(tile == tiles - 1)
    def _():
        wide_ref[pl.ds(HALF + local_cols, HALF)] = jnp.zeros(halo_high.shape, F32)

    @pl.when(tile < tiles - 1)
    def _():
        halo_copy(True).wait_send()

    @pl.when(tile > 0)
    def _():
        halo_copy(False).wait_send()

    for offset in range(1, owners):
        date_copy(offset, me, lax.rem(me + offset, owners)).wait_send()


def filter_kernel(
    wide_ref, coh_in, fch, fcl, frh, frl, box_ref, sum_ref, irh, irl, ich, icl, out_ref, coh_out
):
    coh_out[...] = coh_in[...]
    lanes = wide_ref.shape[1]
    width = frh.shape[1]
    span = fch.shape[0] // 2
    count = span // PATCH
    high, low = split(wide_ref[...])
    part = dot(fch[...], high) + dot(fch[...], low) + dot(fcl[...], high)
    for g in range(lanes // width):
        at = slice(g * width, (g + 1) * width)
        both = jnp.concatenate([part[:span, at], part[span:, at]], axis=1)
        high, low = split(both)
        spec = dot(high, frh[...]) + dot(low, frh[...]) + dot(high, frl[...])
        high, low = split(spec * spec)
        rows = dot(high, box_ref[...]) + dot(low, box_ref[...])
        pieces, totals = [], []
        for k in range(count):
            r = rows[k * PATCH : (k + 1) * PATCH]
            totals.append(jnp.sum(r, axis=0, keepdims=True))
            pieces.append(r + pltpu.roll(r, 1, 0) + pltpu.roll(r, PATCH - 1, 0))
        totals += [jnp.zeros_like(totals[0])] * (-count % 8)
        high, low = split(jnp.concatenate(totals, axis=0))
        level = (dot(high, sum_ref[...]) + dot(low, sum_ref[...])) * (1.0 / (3 * PATCH * PATCH))
        inverse = 1.0 / (level + 1e-6)
        scaled = []
        for k in range(count):
            ratio = (pieces[k] * (1.0 / 9.0) + 0.1 * level[k : k + 1]) * inverse[k : k + 1]
            scaled.append(spec[k * PATCH : (k + 1) * PATCH] * lax.rsqrt(lax.rsqrt(ratio)))
        high, low = split(jnp.concatenate(scaled, axis=0))
        back = dot(high, irh[...]) + dot(low, irh[...]) + dot(high, irl[...])
        high, low = split(jnp.concatenate([back[:, :width], back[:, width:]], axis=0))
        final = dot(ich[...], high) + dot(ich[...], low) + dot(icl[...], high)
        final = final.T
        for p in range(GROUP):
            for c in range(2):
                first = (p * 2 + c) * PATCH
                out_ref[c, g * GROUP + p] = final[first : first + PATCH]


def local(slc, pairs):
    owners = lax.axis_size("date")
    tiles = lax.axis_size("tile")
    rows, cols = slc.shape[2], slc.shape[3]
    looked_cols = cols // RG
    half_rows = rows // AZ
    pair_count = pairs.shape[0] // owners
    lanes = pair_count * 2 * half_rows
    vmem = pl.BlockSpec(memory_space=pltpu.VMEM)
    smem = pl.BlockSpec(memory_space=pltpu.SMEM)
    look = look_table(cols)
    wide, coh = pl.pallas_call(
        functools.partial(gather_kernel, owners, tiles, pair_count),
        out_shape=(
            jax.ShapeDtypeStruct((looked_cols + PATCH, lanes), F32),
            jax.ShapeDtypeStruct((pair_count, half_rows, looked_cols), F32),
        ),
        in_specs=[smem, vmem, vmem, vmem],
        out_specs=(vmem, vmem),
        scratch_shapes=[
            pltpu.VMEM((owners - 1, REQ, 2, cols // LANES, rows, LANES), F32),
            pltpu.VMEM((owners, REQ, 2, cols // LANES, rows, LANES), F32),
            pltpu.SMEM((owners,), jnp.int32),
            pltpu.VMEM((pair_count, 2, half_rows, cols), F32),
            pltpu.VMEM((owners, REQ, half_rows, cols), F32),
            pltpu.VMEM((pair_count, 2, half_rows, looked_cols), F32),
            pltpu.VMEM((owners, REQ, half_rows, looked_cols), F32),
            pltpu.VMEM((looked_cols, lanes), F32),
            pltpu.VMEM((HALF, lanes), F32),
            pltpu.VMEM((HALF, lanes), F32),
            pltpu.SemaphoreType.DMA((owners - 1,)),
            pltpu.SemaphoreType.DMA((owners,)),
            pltpu.SemaphoreType.DMA((2,)),
            pltpu.SemaphoreType.DMA((2,)),
        ],
        compiler_params=pltpu.CompilerParams(
            collective_id=0, has_side_effects=True, vmem_limit_bytes=40 * 2**20
        ),
        name="gather_looks",
    )(pairs, slc, look, np.ascontiguousarray(look.T))
    tables = filter_tables(looked_cols)
    return pl.pallas_call(
        filter_kernel,
        out_shape=(
            jax.ShapeDtypeStruct((2, pair_count, half_rows, looked_cols), F32),
            jax.ShapeDtypeStruct(coh.shape, F32),
        ),
        in_specs=[vmem] * (2 + len(tables)),
        out_specs=(vmem, vmem),
        compiler_params=pltpu.CompilerParams(vmem_limit_bytes=40 * 2**20),
        name="filter_patches",
    )(wide, coh, *tables)


def solution(mesh):
    placed = (P("date", None, "groups", "tile"), P())
    return jax.shard_map(
        local,
        mesh=mesh,
        in_specs=placed,
        out_specs=(P(None, "date", "groups", "tile"), P("date", "groups", "tile")),
        check_vma=False,
    )
```

```python
import functools
import math

import jax
import jax.numpy as jnp
import ml_dtypes
import numpy as np
from jax import lax
from jax.experimental import pallas as pl
from jax.experimental.pallas import tpu as pltpu
from jax.sharding import PartitionSpec as P

REQ = 2
AZ = 2
RG = 4
PATCH = 32
HALF = PATCH // 2
GROUP = 4
LANES = 128
MESH = pl.DeviceIdType.MESH
F32 = jnp.float32
BF16 = jnp.bfloat16


def split(value):
    high = value.astype(BF16)
    low = (value - high.astype(F32)).astype(BF16)
    return high, low


def dot(a, b):
    return jnp.dot(a, b, preferred_element_type=F32)


def dot_nt(a, b):
    return lax.dot_general(a, b, (((1,), (1,)), ((), ())), preferred_element_type=F32)


def np_split(table):
    high = table.astype(np.float32).astype(ml_dtypes.bfloat16)
    low = (table - high.astype(np.float64)).astype(np.float32).astype(ml_dtypes.bfloat16)
    return high, low


def np_round(table):
    return table.astype(np.float32).astype(ml_dtypes.bfloat16)


def look_tables(cols):
    looked = cols // RG
    hit = np.arange(cols)[None, :] // RG == np.arange(looked)[:, None]
    table = np_round(hit / (AZ * RG))
    return np.ascontiguousarray(table[: LANES // RG, :LANES]), np.ascontiguousarray(table.T)


def blocks(small):
    size = small.shape[0] * small.shape[1]
    small = small.reshape(size, size)
    return np.kron(np.eye(GROUP), small)


def three(table):
    high, low = np_split(table)
    return np.concatenate([high, high, low], axis=1)


def filter_tables():
    index = np.arange(PATCH)
    angle = 2.0 * math.pi / PATCH * ((index[:, None] * index[None, :]) % PATCH)
    cos, sin = np.cos(angle), np.sin(angle)
    weight = np.sin(math.pi * (index + 0.5) / PATCH) ** 2 / (PATCH * PATCH)
    fwd_col = np.concatenate([cos, sin], axis=0)
    inv_col = np.concatenate([weight[:, None] * cos, weight[:, None] * sin], axis=1)

    def pair_block(rr, ri, ir, ii):
        small = np.zeros((2, PATCH, 2, PATCH))
        small[0, :, 0], small[0, :, 1], small[1, :, 0], small[1, :, 1] = rr, ri, ir, ii
        return blocks(small)

    fwd_row = np.concatenate(
        [pair_block(cos, -sin, sin, cos), pair_block(-sin, -cos, cos, -sin)], axis=0
    )
    inv_row = np.concatenate(
        [pair_block(cos, sin, -sin, cos), pair_block(-sin, cos, -cos, -sin)], axis=1
    )
    apart = (index[:, None] - index[None, :]) % PATCH
    box = ((apart == 0) | (apart == 1) | (apart == PATCH - 1)).astype(np.float64)
    ones = np.ones((PATCH, PATCH))
    zero = np.zeros((PATCH, PATCH))
    return (
        three(fwd_col),
        *np_split(fwd_row),
        np_round(pair_block(box, box, box, box)),
        np_round(pair_block(ones, zero, zero, ones)),
        *np_split(inv_row),
        three(inv_col),
    )


def triple(value):
    high, low = split(value)
    return jnp.concatenate([high, low, high], axis=0)


def filtered(patches, tables):
    fwd_col, frh, frl, box, ones, irh, irl, inv_col = tables
    width = frh.shape[1]
    groups = patches[0].shape[1] // width
    stacked = []
    for patch in patches:
        part = dot(fwd_col[...], triple(patch))
        for g in range(groups):
            at = slice(g * width, (g + 1) * width)
            stacked.append(jnp.concatenate([part[:PATCH, at], part[PATCH:, at]], axis=1))
    high, low = split(jnp.concatenate(stacked, axis=0))
    spec = dot(high, frh[...]) + dot(low, frh[...]) + dot(high, frl[...])
    high, low = split(spec * spec)
    rows = dot(high, box[...]) + dot(low, box[...])
    count = len(stacked)
    pieces, totals = [], []
    for k in range(count):
        r = rows[k * PATCH : (k + 1) * PATCH]
        totals.append(jnp.sum(r, axis=0, keepdims=True))
        pieces.append(r + pltpu.roll(r, 1, 0) + pltpu.roll(r, PATCH - 1, 0))
    totals += [jnp.zeros_like(totals[0])] * (-count % 8)
    high, low = split(jnp.concatenate(totals, axis=0))
    level = (dot(high, ones[...]) + dot(low, ones[...])) * (1.0 / (3 * PATCH * PATCH))
    inverse = 1.0 / (level + 1e-6)
    scaled = []
    for k in range(count):
        ratio = (pieces[k] * (1.0 / 9.0) + 0.1 * level[k : k + 1]) * inverse[k : k + 1]
        scaled.append(spec[k * PATCH : (k + 1) * PATCH] * lax.rsqrt(lax.rsqrt(ratio)))
    high, low = split(jnp.concatenate(scaled, axis=0))
    back = dot(high, irh[...]) + dot(low, irh[...]) + dot(high, irl[...])
    results = []
    for n in range(len(patches)):
        own = [back[(n * groups + g) * PATCH : (n * groups + g + 1) * PATCH] for g in range(groups)]
        real = jnp.concatenate([b[:, :width] for b in own], axis=1)
        turned = jnp.concatenate([b[:, width:] for b in own], axis=1)
        results.append(dot(inv_col[...], triple(jnp.concatenate([real, turned], axis=0))))
    return results


def gather_kernel(
    owners, tiles, pair_count, table_count,
    pairs_ref, slc_hbm, look_hbm, look_t_hbm, *refs,
):
    tables_hbm, refs = refs[:table_count], refs[table_count:]
    edges_ref, acc_ref, coh_ref = refs[:3]
    tables, refs = refs[3 : 3 + table_count], refs[3 + table_count :]
    chunks = slc_hbm.shape[3] // LANES
    slc_refs, recvs, refs = refs[:chunks], refs[chunks : 2 * chunks], refs[2 * chunks :]
    (
        look_ref, look_t_ref, send, low_tab, prods, powers, natural,
        power_looked, looked, halo_low, halo_high,
        load_sem, send_sem, recv_sem, halo_send_sem, halo_recv_sem,
    ) = refs
    me = lax.axis_index("date")
    tile = lax.axis_index("tile")
    dates_here, _, rows_here, _ = slc_hbm.shape
    half_rows = rows_here // AZ
    local_cols = chunks * LANES // RG
    chunk_cols = LANES // RG

    loads = [
        pltpu.make_async_copy(
            slc_hbm.at[:, :, :, pl.ds(h * LANES, LANES)], slc_refs[h], load_sem.at[h]
        )
        for h in range(chunks)
    ]
    for source, target in zip(
        (look_hbm, look_t_hbm, *tables_hbm), (look_ref, look_t_ref, *tables)
    ):
        loads.append(pltpu.make_async_copy(source, target, load_sem.at[len(loads)]))
    for load in loads[:chunks]:
        load.start()

    barrier = pltpu.get_barrier_semaphore()
    for offset in range(1, owners):
        pl.semaphore_signal(
            barrier, inc=1, device_id={"date": lax.rem(me + offset, owners)}, device_id_type=MESH
        )

    @pl.when(tile > 0)
    def _():
        pl.semaphore_signal(barrier, inc=1, device_id={"tile": tile - 1}, device_id_type=MESH)

    @pl.when(tile < tiles - 1)
    def _():
        pl.semaphore_signal(barrier, inc=1, device_id={"tile": tile + 1}, device_id_type=MESH)

    for load in loads[chunks:]:
        load.start()

    def ends(block, source):
        first = source * dates_here

        def step(i, carry):
            low, high = carry
            for c in range(2):
                date = pairs_ref[c, block * pair_count + i] - first
                inside = (date >= 0) & (date < dates_here)
                low = jnp.where(inside, jnp.minimum(low, date), low)
                high = jnp.where(inside, jnp.maximum(high, date), high)
            return low, high

        return lax.fori_loop(
            0, pair_count, step, (jnp.int32(dates_here - 1), jnp.int32(0)), unroll=True
        )

    def stage(target, h, low, high):
        for rank, pick in ((0, low), (1, high)):
            for part in range(2):
                target[rank, part] = slc_refs[h][pick, part]

    def date_copy(h, offset, source, target):
        return pltpu.make_async_remote_copy(
            src_ref=send.at[h, offset - 1],
            dst_ref=recvs[h].at[source],
            send_sem=send_sem.at[h, offset - 1],
            recv_sem=recv_sem.at[h, source],
            device_id={"date": target},
            device_id_type=MESH,
        )

    picks = [ends(lax.rem(me + offset, owners), me) for offset in range(1, owners)]
    below = lax.div(tile + tiles - 1, tiles)
    above = lax.div(2 * (tiles - 1) - tile, tiles)
    pl.semaphore_wait(barrier, owners - 1 + below + above)
    for h in range(chunks):
        loads[h].wait()
        for offset in range(1, owners):
            stage(send.at[h, offset - 1], h, *picks[offset - 1])
            date_copy(h, offset, me, lax.rem(me + offset, owners)).start()

    low, high = ends(me, me)
    for h in range(chunks):
        stage(recvs[h].at[me], h, low, high)
    for source in range(owners):
        low, _ = ends(me, jnp.int32(source))
        low_tab[source] = low + source * dates_here
    acc_ref[...] = jnp.zeros(acc_ref.shape, F32)
    for load in loads[chunks:]:
        load.wait()

    def slot(i, c):
        date = pairs_ref[c, me * pair_count + i]
        source = lax.div(date, jnp.int32(dates_here))
        rank = jnp.where(date == low_tab[source], 0, 1)
        return source, rank

    def halo_copy(up):
        step = 1 if up else -1
        return pltpu.make_async_remote_copy(
            src_ref=looked.at[pl.ds(local_cols - HALF if up else 0, HALF)],
            dst_ref=halo_low if up else halo_high,
            send_sem=halo_send_sem.at[0 if up else 1],
            recv_sem=halo_recv_sem.at[0 if up else 1],
            device_id={"tile": tile + step},
            device_id_type=MESH,
        )

    for h in range(chunks):
        for offset in range(1, owners):
            source = lax.rem(me + owners - offset, owners)
            date_copy(h, offset, source, source).wait_recv()

        recv = recvs[h]

        def product(i, _):
            sa, ra = slot(i, 0)
            sb, rb = slot(i, 1)
            real = jnp.zeros((half_rows, LANES), F32)
            imag = jnp.zeros((half_rows, LANES), F32)
            for odd in range(AZ):
                rows = pl.ds(odd, half_rows, stride=AZ)
                a0, a1 = recv[sa, ra, 0, rows, :], recv[sa, ra, 1, rows, :]
                b0, b1 = recv[sb, rb, 0, rows, :], recv[sb, rb, 1, rows, :]
                real = real + (a0 * b0 + a1 * b1)
                imag = imag + (a1 * b0 - a0 * b1)
            prods[i, 0] = real
            prods[i, 1] = imag
            return 0

        lax.fori_loop(0, pair_count, product, 0)
        high, low = split(prods[...].reshape(pair_count * 2 * half_rows, LANES))
        table = look_ref[...]
        looked[pl.ds(h * chunk_cols, chunk_cols)] = dot_nt(table, high) + dot_nt(table, low)

        if h == 0:

            @pl.when(tile > 0)
            def _():
                halo_copy(False).start()

        if h == chunks - 1:

            @pl.when(tile < tiles - 1)
            def _():
                halo_copy(True).start()

        table = look_t_ref[pl.ds(h * LANES, LANES)]
        new = (dot(high, table) + dot(low, table)).reshape(natural.shape)
        natural[...] = new if h == 0 else natural[...] + new

        def power(i, _):
            for rank in range(REQ):
                total = jnp.zeros((half_rows, LANES), F32)
                for part in range(2):
                    for odd in range(AZ):
                        field = recv[i, rank, part, pl.ds(odd, half_rows, stride=AZ), :]
                        total = total + field * field
                powers[i, rank] = total
            return 0

        lax.fori_loop(0, owners, power, 0)
        high, low = split(powers[...].reshape(owners * REQ * half_rows, LANES))
        new = (dot(high, table) + dot(low, table)).reshape(power_looked.shape)
        power_looked[...] = new if h == 0 else power_looked[...] + new

        per_chunk = chunk_cols // HALF
        inner = [k for k in range(h * per_chunk, (h + 1) * per_chunk) if k > 0]
        results = filtered([looked[pl.ds((k - 1) * HALF, PATCH)] for k in inner], tables)
        for k, result in zip(inner, results):
            acc_ref[pl.ds((k - 1) * HALF, PATCH)] += result

    def coherence(i, _):
        sa, ra = slot(i, 0)
        sb, rb = slot(i, 1)
        real, imag = natural[i, 0], natural[i, 1]
        coh_ref[i] = (real * real + imag * imag) / (power_looked[sa, ra] * power_looked[sb, rb])
        return 0

    lax.fori_loop(0, pair_count, coherence, 0)
    edges_ref[0, pl.ds(HALF, HALF)] = looked[pl.ds(0, HALF)]
    edges_ref[1, pl.ds(0, HALF)] = looked[pl.ds(local_cols - HALF, HALF)]

    @pl.when(tile > 0)
    def _():
        halo_copy(True).wait_recv()
        edges_ref[0, pl.ds(0, HALF)] = halo_low[...]

    @pl.when(tile == 0)
    def _():
        edges_ref[0, pl.ds(0, HALF)] = jnp.zeros(halo_low.shape, F32)

    @pl.when(tile < tiles - 1)
    def _():
        halo_copy(False).wait_recv()
        edges_ref[1, pl.ds(HALF, HALF)] = halo_high[...]

    @pl.when(tile == tiles - 1)
    def _():
        edges_ref[1, pl.ds(HALF, HALF)] = jnp.zeros(halo_high.shape, F32)

    @pl.when(tile < tiles - 1)
    def _():
        halo_copy(True).wait_send()

    @pl.when(tile > 0)
    def _():
        halo_copy(False).wait_send()

    for h in range(chunks):
        for offset in range(1, owners):
            date_copy(h, offset, me, lax.rem(me + offset, owners)).wait_send()


def filter_kernel(edges_ref, acc_ref, coh_in, *refs):
    tables, (out_ref, coh_out) = refs[:-2], refs[-2:]
    coh_out[...] = coh_in[...]
    first, last = filtered([edges_ref[0], edges_ref[1]], tables)
    final = jnp.concatenate(
        [
            acc_ref[:HALF] + first[HALF:],
            acc_ref[HALF:-HALF],
            acc_ref[-HALF:] + last[:HALF],
        ],
        axis=0,
    ).T
    for p in range(out_ref.shape[1]):
        for c in range(2):
            at = (p * 2 + c) * PATCH
            out_ref[c, p] = final[at : at + PATCH]


def local(slc, pairs):
    owners = lax.axis_size("date")
    tiles = lax.axis_size("tile")
    rows, cols = slc.shape[2], slc.shape[3]
    looked_cols = cols // RG
    half_rows = rows // AZ
    chunks = cols // LANES
    pair_count = pairs.shape[0] // owners
    lanes = pair_count * 2 * half_rows
    vmem = pl.BlockSpec(memory_space=pltpu.VMEM)
    smem = pl.BlockSpec(memory_space=pltpu.SMEM)
    hbm = pl.BlockSpec(memory_space=pl.ANY)
    look, look_t = look_tables(cols)
    tables = filter_tables()
    held = [jax.ShapeDtypeStruct(t.shape, t.dtype) for t in tables]
    outs = pl.pallas_call(
        functools.partial(gather_kernel, owners, tiles, pair_count, len(tables)),
        out_shape=(
            jax.ShapeDtypeStruct((2, PATCH, lanes), F32),
            jax.ShapeDtypeStruct((looked_cols, lanes), F32),
            jax.ShapeDtypeStruct((pair_count, half_rows, looked_cols), F32),
            *held,
        ),
        in_specs=[smem] + [hbm] * (3 + len(tables)),
        out_specs=(vmem,) * (3 + len(tables)),
        scratch_shapes=[
            *[pltpu.VMEM((*slc.shape[:3], LANES), F32)] * chunks,
            *[pltpu.VMEM((owners, REQ, 2, rows, LANES), F32)] * chunks,
            pltpu.VMEM(look.shape, BF16),
            pltpu.VMEM(look_t.shape, BF16),
            pltpu.VMEM((chunks, owners - 1, REQ, 2, rows, LANES), F32),
            pltpu.SMEM((owners,), jnp.int32),
            pltpu.VMEM((pair_count, 2, half_rows, LANES), F32),
            pltpu.VMEM((owners, REQ, half_rows, LANES), F32),
            pltpu.VMEM((pair_count, 2, half_rows, looked_cols), F32),
            pltpu.VMEM((owners, REQ, half_rows, looked_cols), F32),
            pltpu.VMEM((looked_cols, lanes), F32),
            pltpu.VMEM((HALF, lanes), F32),
            pltpu.VMEM((HALF, lanes), F32),
            pltpu.SemaphoreType.DMA((chunks + 2 + len(tables),)),
            pltpu.SemaphoreType.DMA((chunks, owners - 1)),
            pltpu.SemaphoreType.DMA((chunks, owners)),
            pltpu.SemaphoreType.DMA((2,)),
            pltpu.SemaphoreType.DMA((2,)),
        ],
        compiler_params=pltpu.CompilerParams(
            collective_id=0, has_side_effects=True, vmem_limit_bytes=40 * 2**20
        ),
        name="gather_looks",
    )(pairs.T, slc, look, look_t, *tables)
    return pl.pallas_call(
        filter_kernel,
        out_shape=(
            jax.ShapeDtypeStruct((2, pair_count, half_rows, looked_cols), F32),
            jax.ShapeDtypeStruct((pair_count, half_rows, looked_cols), F32),
        ),
        in_specs=[vmem] * len(outs),
        out_specs=(vmem, vmem),
        compiler_params=pltpu.CompilerParams(vmem_limit_bytes=40 * 2**20),
        name="filter_edges",
    )(*outs)


def solution(mesh):
    placed = (P("date", None, "groups", "tile"), P())
    return jax.shard_map(
        local,
        mesh=mesh,
        in_specs=placed,
        out_specs=(P(None, "date", "groups", "tile"), P("date", "groups", "tile")),
        check_vma=False,
    )
```

```python
import functools
import math

import jax
import jax.numpy as jnp
from jax import lax
from jax.experimental import pallas as pl
from jax.experimental.pallas import tpu as pltpu
from jax.sharding import PartitionSpec as P

REQ = 2
AZ = 2
RG = 4
PATCH = 32
HALF = PATCH // 2
GROUP = 4
LANES = 128
MESH = pl.DeviceIdType.MESH
F32 = jnp.float32
BF16 = jnp.bfloat16


def split(value):
    high = value.astype(BF16)
    low = (value - high.astype(F32)).astype(BF16)
    return high, low


def dot(a, b):
    return jnp.dot(a, b, preferred_element_type=F32)


def dot_nt(a, b):
    return lax.dot_general(a, b, (((1,), (1,)), ((), ())), preferred_element_type=F32)


def ids(shape, axis):
    return lax.broadcasted_iota(jnp.int32, shape, axis)


def chosen(index, values):
    result = jnp.zeros(index.shape, F32)
    for i, value in enumerate(values):
        result = jnp.where(index == i, F32(value), result)
    return result


def cos_turn(turn):
    angles = [2.0 * math.pi * i / PATCH for i in range(PATCH)]
    return chosen(turn & (PATCH - 1), [math.cos(a) for a in angles])


def table_shapes():
    width = GROUP * 2 * PATCH
    return (
        (2 * PATCH, 3 * PATCH),
        (2 * width, width),
        (2 * width, width),
        (width, width),
        (width, width),
        (width, 2 * width),
        (width, 2 * width),
        (PATCH, 6 * PATCH),
    )


def fill_tables(look, look_t, fwd_col, frh, frl, box, ones, irh, irl, inv_col):
    quarter = PATCH // 4
    pair = 2 * PATCH
    width = GROUP * pair
    scale = 1.0 / (AZ * RG)
    hit = ids(look.shape, 1) // RG == ids(look.shape, 0)
    look[...] = jnp.where(hit, F32(scale), F32(0.0)).astype(BF16)
    hit = ids(look_t.shape, 0) // RG == ids(look_t.shape, 1)
    look_t[...] = jnp.where(hit, F32(scale), F32(0.0)).astype(BF16)

    row, col = ids(fwd_col.shape, 0), ids(fwd_col.shape, 1)
    value = cos_turn((row & (PATCH - 1)) * (col & (PATCH - 1)) - quarter * (row >> 5))
    high = value.astype(BF16).astype(F32)
    fwd_col[...] = jnp.where(col < 2 * PATCH, high, value - high).astype(BF16)

    row, col = ids(inv_col.shape, 0), ids(inv_col.shape, 1)
    waves = [math.sin(math.pi * (u + 0.5) / PATCH) ** 2 / PATCH**2 for u in range(PATCH)]
    value = chosen(row, waves) * cos_turn(
        row * (col & (PATCH - 1)) - quarter * ((col >> 5) & 1)
    )
    high = value.astype(BF16).astype(F32)
    inv_col[...] = jnp.where(col < 2 * pair, high, value - high).astype(BF16)

    row, col = ids((pair, width), 0), ids((pair, width), 1)
    turn = (row & (PATCH - 1)) * (col & (PATCH - 1))
    lift = quarter * (((col >> 5) & 1) - (row >> 5))
    apart = (row - col) & (PATCH - 1)
    near = (apart == 0) | (apart == 1) | (apart == PATCH - 1)
    same = (row >> 5) == ((col >> 5) & 1)
    for block, turns in enumerate((turn + lift, turn + lift + quarter)):
        value = cos_turn(turns)
        for p in range(GROUP):
            high, low = split(jnp.where(col // pair == p, value, 0.0))
            frh[pl.ds(block * width + p * pair, pair)] = high
            frl[pl.ds(block * width + p * pair, pair)] = low
    for block, turns in enumerate((turn - lift, turn - lift + quarter)):
        value = cos_turn(turns)
        for p in range(GROUP):
            high, low = split(jnp.where(col // pair == p, value, 0.0))
            irh[pl.ds(p * pair, pair), pl.ds(block * width, width)] = high
            irl[pl.ds(p * pair, pair), pl.ds(block * width, width)] = low
    for p in range(GROUP):
        own = col // pair == p
        box[pl.ds(p * pair, pair)] = jnp.where(own & near, F32(1.0), F32(0.0)).astype(BF16)
        ones[pl.ds(p * pair, pair)] = jnp.where(own & same, F32(1.0), F32(0.0)).astype(BF16)


def triple(value):
    high, low = split(value)
    return jnp.concatenate([high, low, high], axis=0)


def filtered(patches, tables):
    fwd_col, frh, frl, box, ones, irh, irl, inv_col = tables
    width = frh.shape[1]
    groups = patches[0].shape[1] // width
    stacked = []
    for patch in patches:
        part = dot(fwd_col[...], triple(patch))
        for g in range(groups):
            at = slice(g * width, (g + 1) * width)
            stacked.append(jnp.concatenate([part[:PATCH, at], part[PATCH:, at]], axis=1))
    high, low = split(jnp.concatenate(stacked, axis=0))
    spec = dot(high, frh[...]) + dot(low, frh[...]) + dot(high, frl[...])
    high, low = split(spec * spec)
    rows = dot(high, box[...]) + dot(low, box[...])
    count = len(stacked)
    pieces, totals = [], []
    for k in range(count):
        r = rows[k * PATCH : (k + 1) * PATCH]
        totals.append(jnp.sum(r, axis=0, keepdims=True))
        pieces.append(r + pltpu.roll(r, 1, 0) + pltpu.roll(r, PATCH - 1, 0))
    totals += [jnp.zeros_like(totals[0])] * (-count % 8)
    high, low = split(jnp.concatenate(totals, axis=0))
    level = (dot(high, ones[...]) + dot(low, ones[...])) * (1.0 / (3 * PATCH * PATCH))
    inverse = 1.0 / (level + 1e-6)
    scaled = []
    for k in range(count):
        ratio = (pieces[k] * (1.0 / 9.0) + 0.1 * level[k : k + 1]) * inverse[k : k + 1]
        scaled.append(spec[k * PATCH : (k + 1) * PATCH] * lax.rsqrt(lax.rsqrt(ratio)))
    high, low = split(jnp.concatenate(scaled, axis=0))
    back = dot(high, irh[...]) + dot(low, irh[...]) + dot(high, irl[...])
    results = []
    for n in range(len(patches)):
        own = [back[(n * groups + g) * PATCH : (n * groups + g + 1) * PATCH] for g in range(groups)]
        real = jnp.concatenate([b[:, :width] for b in own], axis=1)
        turned = jnp.concatenate([b[:, width:] for b in own], axis=1)
        results.append(dot(inv_col[...], triple(jnp.concatenate([real, turned], axis=0))))
    return results


def gather_kernel(
    owners, tiles, pair_count, table_count, pairs_ref, slc_hbm, *refs
):
    edges_ref, acc_ref, coh_ref = refs[:3]
    tables, refs = refs[3 : 3 + table_count], refs[3 + table_count :]
    chunks = slc_hbm.shape[3] // LANES
    slc_refs, recvs, refs = refs[:chunks], refs[chunks : 2 * chunks], refs[2 * chunks :]
    (
        look_ref, look_t_ref, send, low_tab, prods, powers, natural,
        power_looked, looked, halo_low, halo_high,
        load_sem, send_sem, recv_sem, halo_send_sem, halo_recv_sem,
    ) = refs
    me = lax.axis_index("date")
    tile = lax.axis_index("tile")
    dates_here, _, rows_here, _ = slc_hbm.shape
    half_rows = rows_here // AZ
    local_cols = chunks * LANES // RG
    chunk_cols = LANES // RG

    loads = [
        pltpu.make_async_copy(
            slc_hbm.at[:, :, :, pl.ds(h * LANES, LANES)], slc_refs[h], load_sem.at[h]
        )
        for h in range(chunks)
    ]
    for load in loads:
        load.start()

    barrier = pltpu.get_barrier_semaphore()
    for offset in range(1, owners):
        pl.semaphore_signal(
            barrier, inc=1, device_id={"date": lax.rem(me + offset, owners)}, device_id_type=MESH
        )

    @pl.when(tile > 0)
    def _():
        pl.semaphore_signal(barrier, inc=1, device_id={"tile": tile - 1}, device_id_type=MESH)

    @pl.when(tile < tiles - 1)
    def _():
        pl.semaphore_signal(barrier, inc=1, device_id={"tile": tile + 1}, device_id_type=MESH)

    def ends(block, source):
        first = source * dates_here

        def step(i, carry):
            low, high = carry
            for c in range(2):
                date = pairs_ref[c, block * pair_count + i] - first
                inside = (date >= 0) & (date < dates_here)
                low = jnp.where(inside, jnp.minimum(low, date), low)
                high = jnp.where(inside, jnp.maximum(high, date), high)
            return low, high

        return lax.fori_loop(
            0, pair_count, step, (jnp.int32(dates_here - 1), jnp.int32(0)), unroll=True
        )

    def stage(target, h, low, high):
        for rank, pick in ((0, low), (1, high)):
            for part in range(2):
                target[rank, part] = slc_refs[h][pick, part]

    def date_copy(h, offset, source, target):
        return pltpu.make_async_remote_copy(
            src_ref=send.at[h, offset - 1],
            dst_ref=recvs[h].at[source],
            send_sem=send_sem.at[h, offset - 1],
            recv_sem=recv_sem.at[h, source],
            device_id={"date": target},
            device_id_type=MESH,
        )

    picks = [ends(lax.rem(me + offset, owners), me) for offset in range(1, owners)]
    below = lax.div(tile + tiles - 1, tiles)
    above = lax.div(2 * (tiles - 1) - tile, tiles)
    pl.semaphore_wait(barrier, owners - 1 + below + above)
    for h in range(chunks):
        loads[h].wait()
        for offset in range(1, owners):
            stage(send.at[h, offset - 1], h, *picks[offset - 1])
            date_copy(h, offset, me, lax.rem(me + offset, owners)).start()

    low, high = ends(me, me)
    for h in range(chunks):
        stage(recvs[h].at[me], h, low, high)
    for source in range(owners):
        low, _ = ends(me, jnp.int32(source))
        low_tab[source] = low + source * dates_here
    acc_ref[...] = jnp.zeros(acc_ref.shape, F32)
    fill_tables(look_ref, look_t_ref, *tables)

    def slot(i, c):
        date = pairs_ref[c, me * pair_count + i]
        source = lax.div(date, jnp.int32(dates_here))
        rank = jnp.where(date == low_tab[source], 0, 1)
        return source, rank

    def halo_copy(up):
        step = 1 if up else -1
        return pltpu.make_async_remote_copy(
            src_ref=looked.at[pl.ds(local_cols - HALF if up else 0, HALF)],
            dst_ref=halo_low if up else halo_high,
            send_sem=halo_send_sem.at[0 if up else 1],
            recv_sem=halo_recv_sem.at[0 if up else 1],
            device_id={"tile": tile + step},
            device_id_type=MESH,
        )

    for h in range(chunks):
        for offset in range(1, owners):
            source = lax.rem(me + owners - offset, owners)
            date_copy(h, offset, source, source).wait_recv()

        recv = recvs[h]

        def product(i, _):
            sa, ra = slot(i, 0)
            sb, rb = slot(i, 1)
            real = jnp.zeros((half_rows, LANES), F32)
            imag = jnp.zeros((half_rows, LANES), F32)
            for odd in range(AZ):
                rows = pl.ds(odd, half_rows, stride=AZ)
                a0, a1 = recv[sa, ra, 0, rows, :], recv[sa, ra, 1, rows, :]
                b0, b1 = recv[sb, rb, 0, rows, :], recv[sb, rb, 1, rows, :]
                real = real + (a0 * b0 + a1 * b1)
                imag = imag + (a1 * b0 - a0 * b1)
            prods[i, 0] = real
            prods[i, 1] = imag
            return 0

        lax.fori_loop(0, pair_count, product, 0)
        high, low = split(prods[...].reshape(pair_count * 2 * half_rows, LANES))
        table = look_ref[...]
        looked[pl.ds(h * chunk_cols, chunk_cols)] = dot_nt(table, high) + dot_nt(table, low)

        if h == 0:

            @pl.when(tile > 0)
            def _():
                halo_copy(False).start()

        if h == chunks - 1:

            @pl.when(tile < tiles - 1)
            def _():
                halo_copy(True).start()

        table = look_t_ref[pl.ds(h * LANES, LANES)]
        new = (dot(high, table) + dot(low, table)).reshape(natural.shape)
        natural[...] = new if h == 0 else natural[...] + new

        def power(i, _):
            for rank in range(REQ):
                total = jnp.zeros((half_rows, LANES), F32)
                for part in range(2):
                    for odd in range(AZ):
                        field = recv[i, rank, part, pl.ds(odd, half_rows, stride=AZ), :]
                        total = total + field * field
                powers[i, rank] = total
            return 0

        lax.fori_loop(0, owners, power, 0)
        high, low = split(powers[...].reshape(owners * REQ * half_rows, LANES))
        new = (dot(high, table) + dot(low, table)).reshape(power_looked.shape)
        power_looked[...] = new if h == 0 else power_looked[...] + new

        per_chunk = chunk_cols // HALF
        inner = [k for k in range(h * per_chunk, (h + 1) * per_chunk) if k > 0]
        results = filtered([looked[pl.ds((k - 1) * HALF, PATCH)] for k in inner], tables)
        for k, result in zip(inner, results):
            acc_ref[pl.ds((k - 1) * HALF, PATCH)] += result

    def coherence(i, _):
        sa, ra = slot(i, 0)
        sb, rb = slot(i, 1)
        real, imag = natural[i, 0], natural[i, 1]
        coh_ref[i] = (real * real + imag * imag) / (power_looked[sa, ra] * power_looked[sb, rb])
        return 0

    lax.fori_loop(0, pair_count, coherence, 0)
    edges_ref[0, pl.ds(HALF, HALF)] = looked[pl.ds(0, HALF)]
    edges_ref[1, pl.ds(0, HALF)] = looked[pl.ds(local_cols - HALF, HALF)]

    @pl.when(tile > 0)
    def _():
        halo_copy(True).wait_recv()
        edges_ref[0, pl.ds(0, HALF)] = halo_low[...]

    @pl.when(tile == 0)
    def _():
        edges_ref[0, pl.ds(0, HALF)] = jnp.zeros(halo_low.shape, F32)

    @pl.when(tile < tiles - 1)
    def _():
        halo_copy(False).wait_recv()
        edges_ref[1, pl.ds(HALF, HALF)] = halo_high[...]

    @pl.when(tile == tiles - 1)
    def _():
        edges_ref[1, pl.ds(HALF, HALF)] = jnp.zeros(halo_high.shape, F32)

    @pl.when(tile < tiles - 1)
    def _():
        halo_copy(True).wait_send()

    @pl.when(tile > 0)
    def _():
        halo_copy(False).wait_send()

    for h in range(chunks):
        for offset in range(1, owners):
            date_copy(h, offset, me, lax.rem(me + offset, owners)).wait_send()


def filter_kernel(edges_ref, acc_ref, coh_in, *refs):
    tables, (out_ref, coh_out) = refs[:-2], refs[-2:]
    coh_out[...] = coh_in[...]
    first, last = filtered([edges_ref[0], edges_ref[1]], tables)
    final = jnp.concatenate(
        [
            acc_ref[:HALF] + first[HALF:],
            acc_ref[HALF:-HALF],
            acc_ref[-HALF:] + last[:HALF],
        ],
        axis=0,
    ).T
    for p in range(out_ref.shape[1]):
        for c in range(2):
            at = (p * 2 + c) * PATCH
            out_ref[c, p] = final[at : at + PATCH]


def local(slc, pairs):
    owners = lax.axis_size("date")
    tiles = lax.axis_size("tile")
    rows, cols = slc.shape[2], slc.shape[3]
    looked_cols = cols // RG
    half_rows = rows // AZ
    chunks = cols // LANES
    pair_count = pairs.shape[0] // owners
    lanes = pair_count * 2 * half_rows
    vmem = pl.BlockSpec(memory_space=pltpu.VMEM)
    smem = pl.BlockSpec(memory_space=pltpu.SMEM)
    hbm = pl.BlockSpec(memory_space=pltpu.HBM)
    tables = [jax.ShapeDtypeStruct(shape, BF16) for shape in table_shapes()]
    outs = pl.pallas_call(
        functools.partial(gather_kernel, owners, tiles, pair_count, len(tables)),
        out_shape=(
            jax.ShapeDtypeStruct((2, PATCH, lanes), F32),
            jax.ShapeDtypeStruct((looked_cols, lanes), F32),
            jax.ShapeDtypeStruct((pair_count, half_rows, looked_cols), F32),
            *tables,
        ),
        in_specs=[smem, hbm],
        out_specs=(vmem,) * (3 + len(tables)),
        scratch_shapes=[
            *[pltpu.VMEM((*slc.shape[:3], LANES), F32)] * chunks,
            *[pltpu.VMEM((owners, REQ, 2, rows, LANES), F32)] * chunks,
            pltpu.VMEM((LANES // RG, LANES), BF16),
            pltpu.VMEM((cols, looked_cols), BF16),
            pltpu.VMEM((chunks, owners - 1, REQ, 2, rows, LANES), F32),
            pltpu.SMEM((owners,), jnp.int32),
            pltpu.VMEM((pair_count, 2, half_rows, LANES), F32),
            pltpu.VMEM((owners, REQ, half_rows, LANES), F32),
            pltpu.VMEM((pair_count, 2, half_rows, looked_cols), F32),
            pltpu.VMEM((owners, REQ, half_rows, looked_cols), F32),
            pltpu.VMEM((looked_cols, lanes), F32),
            pltpu.VMEM((HALF, lanes), F32),
            pltpu.VMEM((HALF, lanes), F32),
            pltpu.SemaphoreType.DMA((chunks,)),
            pltpu.SemaphoreType.DMA((chunks, owners - 1)),
            pltpu.SemaphoreType.DMA((chunks, owners)),
            pltpu.SemaphoreType.DMA((2,)),
            pltpu.SemaphoreType.DMA((2,)),
        ],
        compiler_params=pltpu.CompilerParams(
            collective_id=0, has_side_effects=True, vmem_limit_bytes=40 * 2**20
        ),
        name="gather_looks",
    )(pairs.T, slc)
    return pl.pallas_call(
        filter_kernel,
        out_shape=(
            jax.ShapeDtypeStruct((2, pair_count, half_rows, looked_cols), F32),
            jax.ShapeDtypeStruct((pair_count, half_rows, looked_cols), F32),
        ),
        in_specs=[vmem] * len(outs),
        out_specs=(vmem, vmem),
        compiler_params=pltpu.CompilerParams(vmem_limit_bytes=40 * 2**20),
        name="filter_edges",
    )(*outs)


def solution(mesh):
    placed = (P("date", None, "groups", "tile"), P())
    return jax.shard_map(
        local,
        mesh=mesh,
        in_specs=placed,
        out_specs=(P(None, "date", "groups", "tile"), P("date", "groups", "tile")),
        check_vma=False,
    )
```

```python
import functools
import math

import jax
import jax.numpy as jnp
from jax import lax
from jax.experimental import pallas as pl
from jax.experimental.pallas import tpu as pltpu
from jax.sharding import PartitionSpec as P

REQ = 2
AZ = 2
RG = 4
PATCH = 32
HALF = PATCH // 2
GROUP = 4
LANES = 128
MESH = pl.DeviceIdType.MESH
F32 = jnp.float32
BF16 = jnp.bfloat16


def split(value):
    high = value.astype(BF16)
    low = (value - high.astype(F32)).astype(BF16)
    return high, low


def dot(a, b):
    return jnp.dot(a, b, preferred_element_type=F32)


def dot_nt(a, b):
    return lax.dot_general(a, b, (((1,), (1,)), ((), ())), preferred_element_type=F32)


def ids(shape, axis):
    return lax.broadcasted_iota(jnp.int32, shape, axis)


def chosen(index, values):
    result = jnp.zeros(index.shape, F32)
    for i, value in enumerate(values):
        result = jnp.where(index == i, F32(value), result)
    return result


def cos_turn(turn):
    angles = [2.0 * math.pi * i / PATCH for i in range(PATCH)]
    return chosen(turn & (PATCH - 1), [math.cos(a) for a in angles])


def table_shapes():
    width = GROUP * 2 * PATCH
    return (
        (2 * PATCH, 3 * PATCH),
        (2 * width, width),
        (2 * width, width),
        (width, width),
        (width, width),
        (width, 2 * width),
        (width, 2 * width),
        (PATCH, 6 * PATCH),
    )


def fill_tables(look, look_t, fwd_col, frh, frl, box, ones, irh, irl, inv_col):
    quarter = PATCH // 4
    pair = 2 * PATCH
    width = GROUP * pair
    scale = 1.0 / (AZ * RG)
    hit = ids(look.shape, 1) // RG == ids(look.shape, 0)
    look[...] = jnp.where(hit, F32(scale), F32(0.0)).astype(BF16)
    hit = ids(look_t.shape, 0) // RG == ids(look_t.shape, 1)
    look_t[...] = jnp.where(hit, F32(scale), F32(0.0)).astype(BF16)

    row, col = ids(fwd_col.shape, 0), ids(fwd_col.shape, 1)
    value = cos_turn((row & (PATCH - 1)) * (col & (PATCH - 1)) - quarter * (row >> 5))
    high = value.astype(BF16).astype(F32)
    fwd_col[...] = jnp.where(col < 2 * PATCH, high, value - high).astype(BF16)

    row, col = ids(inv_col.shape, 0), ids(inv_col.shape, 1)
    waves = [math.sin(math.pi * (u + 0.5) / PATCH) ** 2 / PATCH**2 for u in range(PATCH)]
    value = chosen(row, waves) * cos_turn(
        row * (col & (PATCH - 1)) - quarter * ((col >> 5) & 1)
    )
    high = value.astype(BF16).astype(F32)
    inv_col[...] = jnp.where(col < 2 * pair, high, value - high).astype(BF16)

    row, col = ids((pair, width), 0), ids((pair, width), 1)
    turn = (row & (PATCH - 1)) * (col & (PATCH - 1))
    lift = quarter * (((col >> 5) & 1) - (row >> 5))
    apart = (row - col) & (PATCH - 1)
    near = (apart == 0) | (apart == 1) | (apart == PATCH - 1)
    same = (row >> 5) == ((col >> 5) & 1)
    for block, turns in enumerate((turn + lift, turn + lift + quarter)):
        value = cos_turn(turns)
        for p in range(GROUP):
            high, low = split(jnp.where(col // pair == p, value, 0.0))
            frh[pl.ds(block * width + p * pair, pair)] = high
            frl[pl.ds(block * width + p * pair, pair)] = low
    for block, turns in enumerate((turn - lift, turn - lift + quarter)):
        value = cos_turn(turns)
        for p in range(GROUP):
            high, low = split(jnp.where(col // pair == p, value, 0.0))
            irh[pl.ds(p * pair, pair), pl.ds(block * width, width)] = high
            irl[pl.ds(p * pair, pair), pl.ds(block * width, width)] = low
    for p in range(GROUP):
        own = col // pair == p
        box[pl.ds(p * pair, pair)] = jnp.where(own & near, F32(1.0), F32(0.0)).astype(BF16)
        ones[pl.ds(p * pair, pair)] = jnp.where(own & same, F32(1.0), F32(0.0)).astype(BF16)


def triple(value):
    high, low = split(value)
    return jnp.concatenate([high, low, high], axis=0)


def filtered(patches, tables):
    fwd_col, frh, frl, box, ones, irh, irl, inv_col = tables
    width = frh.shape[1]
    groups = patches[0].shape[1] // width
    stacked = []
    for patch in patches:
        part = dot(fwd_col[...], triple(patch))
        for g in range(groups):
            at = slice(g * width, (g + 1) * width)
            stacked.append(jnp.concatenate([part[:PATCH, at], part[PATCH:, at]], axis=1))
    high, low = split(jnp.concatenate(stacked, axis=0))
    spec = dot(high, frh[...]) + dot(low, frh[...]) + dot(high, frl[...])
    high, low = split(spec * spec)
    rows = dot(high, box[...]) + dot(low, box[...])
    count = len(stacked)
    pieces, totals = [], []
    for k in range(count):
        r = rows[k * PATCH : (k + 1) * PATCH]
        totals.append(jnp.sum(r, axis=0, keepdims=True))
        pieces.append(r + pltpu.roll(r, 1, 0) + pltpu.roll(r, PATCH - 1, 0))
    totals += [jnp.zeros_like(totals[0])] * (-count % 8)
    high, low = split(jnp.concatenate(totals, axis=0))
    level = (dot(high, ones[...]) + dot(low, ones[...])) * (1.0 / (3 * PATCH * PATCH))
    inverse = 1.0 / (level + 1e-6)
    scaled = []
    for k in range(count):
        ratio = (pieces[k] * (1.0 / 9.0) + 0.1 * level[k : k + 1]) * inverse[k : k + 1]
        scaled.append(spec[k * PATCH : (k + 1) * PATCH] * lax.rsqrt(lax.rsqrt(ratio)))
    high, low = split(jnp.concatenate(scaled, axis=0))
    back = dot(high, irh[...]) + dot(low, irh[...]) + dot(high, irl[...])
    results = []
    for n in range(len(patches)):
        own = [back[(n * groups + g) * PATCH : (n * groups + g + 1) * PATCH] for g in range(groups)]
        real = jnp.concatenate([b[:, :width] for b in own], axis=1)
        turned = jnp.concatenate([b[:, width:] for b in own], axis=1)
        results.append(dot(inv_col[...], triple(jnp.concatenate([real, turned], axis=0))))
    return results


def gather_kernel(
    owners, tiles, pair_count, table_count, pairs_ref, slc_ref, *refs
):
    edges_ref, acc_ref, coh_ref = refs[:3]
    tables, refs = refs[3 : 3 + table_count], refs[3 + table_count :]
    chunks = slc_ref.shape[3] // LANES
    recvs, refs = refs[:chunks], refs[chunks:]
    (
        look_ref, look_t_ref, send, low_tab, slots, prods, powers, natural,
        power_looked, looked, halo_low, halo_high,
        send_sem, recv_sem, halo_send_sem, halo_recv_sem,
    ) = refs
    me = lax.axis_index("date")
    tile = lax.axis_index("tile")
    dates_here, _, rows_here, _ = slc_ref.shape
    half_rows = rows_here // AZ
    local_cols = chunks * LANES // RG
    chunk_cols = LANES // RG

    barrier = pltpu.get_barrier_semaphore()
    for offset in range(1, owners):
        pl.semaphore_signal(
            barrier, inc=1, device_id={"date": lax.rem(me + offset, owners)}, device_id_type=MESH
        )

    @pl.when(tile > 0)
    def _():
        pl.semaphore_signal(barrier, inc=1, device_id={"tile": tile - 1}, device_id_type=MESH)

    @pl.when(tile < tiles - 1)
    def _():
        pl.semaphore_signal(barrier, inc=1, device_id={"tile": tile + 1}, device_id_type=MESH)

    def ends(block, source):
        first = source * dates_here

        def step(i, carry):
            low, high = carry
            for c in range(2):
                date = pairs_ref[c, block * pair_count + i] - first
                inside = (date >= 0) & (date < dates_here)
                low = jnp.where(inside, jnp.minimum(low, date), low)
                high = jnp.where(inside, jnp.maximum(high, date), high)
            return low, high

        return lax.fori_loop(
            0, pair_count, step, (jnp.int32(dates_here - 1), jnp.int32(0)), unroll=True
        )

    def stage(target, h, low, high):
        for rank, pick in ((0, low), (1, high)):
            for part in range(2):
                target[rank, part] = slc_ref[pick, part, :, h * LANES : (h + 1) * LANES]

    def date_copy(h, offset, source, target):
        return pltpu.make_async_remote_copy(
            src_ref=send.at[h, offset - 1],
            dst_ref=recvs[h].at[source],
            send_sem=send_sem.at[h, offset - 1],
            recv_sem=recv_sem.at[h, source],
            device_id={"date": target},
            device_id_type=MESH,
        )

    below = lax.div(tile + tiles - 1, tiles)
    above = lax.div(2 * (tiles - 1) - tile, tiles)
    order = sorted(range(1, owners), key=lambda offset: abs(2 * offset - owners))
    picks = {}
    for h in range(chunks):
        for offset in order:
            target = lax.rem(me + offset, owners)
            if h == 0:
                picks[offset] = ends(target, me)
            stage(send.at[h, offset - 1], h, *picks[offset])
            if h == 0 and offset == order[0]:
                pl.semaphore_wait(barrier, owners - 1 + below + above)
            date_copy(h, offset, me, target).start()

    low, high = ends(me, me)
    for h in range(chunks):
        stage(recvs[h].at[me], h, low, high)
    for source in range(owners):
        low, _ = ends(me, jnp.int32(source))
        low_tab[source] = low + source * dates_here
    acc_ref[...] = jnp.zeros(acc_ref.shape, F32)
    fill_tables(look_ref, look_t_ref, *tables)

    def find(i, _):
        for c in range(2):
            date = pairs_ref[c, me * pair_count + i]
            source = lax.div(date, jnp.int32(dates_here))
            slots[2 * c, i] = source
            slots[2 * c + 1, i] = jnp.where(date == low_tab[source], 0, 1)
        return 0

    lax.fori_loop(0, pair_count, find, 0)

    def slot(i, c):
        return slots[2 * c, i], slots[2 * c + 1, i]

    def halo_copy(up):
        step = 1 if up else -1
        return pltpu.make_async_remote_copy(
            src_ref=looked.at[pl.ds(local_cols - HALF if up else 0, HALF)],
            dst_ref=halo_low if up else halo_high,
            send_sem=halo_send_sem.at[0 if up else 1],
            recv_sem=halo_recv_sem.at[0 if up else 1],
            device_id={"tile": tile + step},
            device_id_type=MESH,
        )

    for h in range(chunks):
        for offset in range(1, owners):
            source = lax.rem(me + owners - offset, owners)
            date_copy(h, offset, source, source).wait_recv()

        recv = recvs[h]

        def product(i, _):
            sa, ra = slot(i, 0)
            sb, rb = slot(i, 1)
            real = jnp.zeros((half_rows, LANES), F32)
            imag = jnp.zeros((half_rows, LANES), F32)
            for odd in range(AZ):
                rows = pl.ds(odd, half_rows, stride=AZ)
                a0, a1 = recv[sa, ra, 0, rows, :], recv[sa, ra, 1, rows, :]
                b0, b1 = recv[sb, rb, 0, rows, :], recv[sb, rb, 1, rows, :]
                real = real + (a0 * b0 + a1 * b1)
                imag = imag + (a1 * b0 - a0 * b1)
            prods[i, 0] = real
            prods[i, 1] = imag
            return 0

        lax.fori_loop(0, pair_count, product, 0, unroll=4)
        high, low = split(prods[...].reshape(pair_count * 2 * half_rows, LANES))
        table = look_ref[...]
        looked[pl.ds(h * chunk_cols, chunk_cols)] = dot_nt(table, high) + dot_nt(table, low)

        if h == 0:

            @pl.when(tile > 0)
            def _():
                halo_copy(False).start()

        if h == chunks - 1:

            @pl.when(tile < tiles - 1)
            def _():
                halo_copy(True).start()

        table = look_t_ref[pl.ds(h * LANES, LANES)]
        new = (dot(high, table) + dot(low, table)).reshape(natural.shape)
        natural[...] = new if h == 0 else natural[...] + new

        def power(i, _):
            for rank in range(REQ):
                total = jnp.zeros((half_rows, LANES), F32)
                for part in range(2):
                    for odd in range(AZ):
                        field = recv[i, rank, part, pl.ds(odd, half_rows, stride=AZ), :]
                        total = total + field * field
                powers[i, rank] = total
            return 0

        lax.fori_loop(0, owners, power, 0, unroll=2)
        high, low = split(powers[...].reshape(owners * REQ * half_rows, LANES))
        new = (dot(high, table) + dot(low, table)).reshape(power_looked.shape)
        power_looked[...] = new if h == 0 else power_looked[...] + new

        per_chunk = chunk_cols // HALF
        inner = [k for k in range(h * per_chunk, (h + 1) * per_chunk) if k > 0]
        results = filtered([looked[pl.ds((k - 1) * HALF, PATCH)] for k in inner], tables)
        for k, result in zip(inner, results):
            acc_ref[pl.ds((k - 1) * HALF, PATCH)] += result

    def coherence(i, _):
        sa, ra = slot(i, 0)
        sb, rb = slot(i, 1)
        real, imag = natural[i, 0], natural[i, 1]
        coh_ref[i] = (real * real + imag * imag) / (power_looked[sa, ra] * power_looked[sb, rb])
        return 0

    lax.fori_loop(0, pair_count, coherence, 0, unroll=4)
    edges_ref[0, pl.ds(HALF, HALF)] = looked[pl.ds(0, HALF)]
    edges_ref[1, pl.ds(0, HALF)] = looked[pl.ds(local_cols - HALF, HALF)]

    @pl.when(tile > 0)
    def _():
        halo_copy(True).wait_recv()
        edges_ref[0, pl.ds(0, HALF)] = halo_low[...]

    @pl.when(tile == 0)
    def _():
        edges_ref[0, pl.ds(0, HALF)] = jnp.zeros(halo_low.shape, F32)

    @pl.when(tile < tiles - 1)
    def _():
        halo_copy(False).wait_recv()
        edges_ref[1, pl.ds(HALF, HALF)] = halo_high[...]

    @pl.when(tile == tiles - 1)
    def _():
        edges_ref[1, pl.ds(HALF, HALF)] = jnp.zeros(halo_high.shape, F32)

    @pl.when(tile < tiles - 1)
    def _():
        halo_copy(True).wait_send()

    @pl.when(tile > 0)
    def _():
        halo_copy(False).wait_send()

    for h in range(chunks):
        for offset in range(1, owners):
            date_copy(h, offset, me, lax.rem(me + offset, owners)).wait_send()


def filter_kernel(edges_ref, acc_ref, coh_in, *refs):
    tables, (out_ref, coh_out) = refs[:-2], refs[-2:]
    coh_out[...] = coh_in[...]
    first, last = filtered([edges_ref[0], edges_ref[1]], tables)
    final = jnp.concatenate(
        [
            acc_ref[:HALF] + first[HALF:],
            acc_ref[HALF:-HALF],
            acc_ref[-HALF:] + last[:HALF],
        ],
        axis=0,
    ).T
    for p in range(out_ref.shape[1]):
        for c in range(2):
            at = (p * 2 + c) * PATCH
            out_ref[c, p] = final[at : at + PATCH]


def local(slc, pairs):
    owners = lax.axis_size("date")
    tiles = lax.axis_size("tile")
    rows, cols = slc.shape[2], slc.shape[3]
    looked_cols = cols // RG
    half_rows = rows // AZ
    chunks = cols // LANES
    pair_count = pairs.shape[0] // owners
    lanes = pair_count * 2 * half_rows
    vmem = pl.BlockSpec(memory_space=pltpu.VMEM)
    smem = pl.BlockSpec(memory_space=pltpu.SMEM)
    tables = [jax.ShapeDtypeStruct(shape, BF16) for shape in table_shapes()]
    outs = pl.pallas_call(
        functools.partial(gather_kernel, owners, tiles, pair_count, len(tables)),
        out_shape=(
            jax.ShapeDtypeStruct((2, PATCH, lanes), F32),
            jax.ShapeDtypeStruct((looked_cols, lanes), F32),
            jax.ShapeDtypeStruct((pair_count, half_rows, looked_cols), F32),
            *tables,
        ),
        in_specs=[smem, vmem],
        out_specs=(vmem,) * (3 + len(tables)),
        scratch_shapes=[
            *[pltpu.VMEM((owners, REQ, 2, rows, LANES), F32)] * chunks,
            pltpu.VMEM((LANES // RG, LANES), BF16),
            pltpu.VMEM((cols, looked_cols), BF16),
            pltpu.VMEM((chunks, owners - 1, REQ, 2, rows, LANES), F32),
            pltpu.SMEM((owners,), jnp.int32),
            pltpu.SMEM((4, pair_count), jnp.int32),
            pltpu.VMEM((pair_count, 2, half_rows, LANES), F32),
            pltpu.VMEM((owners, REQ, half_rows, LANES), F32),
            pltpu.VMEM((pair_count, 2, half_rows, looked_cols), F32),
            pltpu.VMEM((owners, REQ, half_rows, looked_cols), F32),
            pltpu.VMEM((looked_cols, lanes), F32),
            pltpu.VMEM((HALF, lanes), F32),
            pltpu.VMEM((HALF, lanes), F32),
            pltpu.SemaphoreType.DMA((chunks, owners - 1)),
            pltpu.SemaphoreType.DMA((chunks, owners)),
            pltpu.SemaphoreType.DMA((2,)),
            pltpu.SemaphoreType.DMA((2,)),
        ],
        compiler_params=pltpu.CompilerParams(
            collective_id=0, has_side_effects=True, vmem_limit_bytes=40 * 2**20
        ),
        name="gather_looks",
    )(pairs.T, slc)
    return pl.pallas_call(
        filter_kernel,
        out_shape=(
            jax.ShapeDtypeStruct((2, pair_count, half_rows, looked_cols), F32),
            jax.ShapeDtypeStruct((pair_count, half_rows, looked_cols), F32),
        ),
        in_specs=[vmem] * len(outs),
        out_specs=(vmem, vmem),
        compiler_params=pltpu.CompilerParams(vmem_limit_bytes=40 * 2**20),
        name="filter_edges",
    )(*outs)


def solution(mesh):
    placed = (P("date", None, "groups", "tile"), P())
    return jax.shard_map(
        local,
        mesh=mesh,
        in_specs=placed,
        out_specs=(P(None, "date", "groups", "tile"), P("date", "groups", "tile")),
        check_vma=False,
    )
```

```python
import functools
import math

import jax
import jax.numpy as jnp
from jax import lax
from jax.experimental import pallas as pl
from jax.experimental.pallas import tpu as pltpu
from jax.sharding import PartitionSpec as P

REQ = 2
AZ = 2
RG = 4
PATCH = 32
HALF = PATCH // 2
GROUP = 4
LANES = 128
MESH = pl.DeviceIdType.MESH
F32 = jnp.float32
BF16 = jnp.bfloat16


def split(value):
    high = value.astype(BF16)
    low = (value - high.astype(F32)).astype(BF16)
    return high, low


def dot(a, b):
    return jnp.dot(a, b, preferred_element_type=F32)


def dot_nt(a, b):
    return lax.dot_general(a, b, (((1,), (1,)), ((), ())), preferred_element_type=F32)


def ids(shape, axis):
    return lax.broadcasted_iota(jnp.int32, shape, axis)


def chosen(index, values):
    result = jnp.zeros(index.shape, F32)
    for i, value in enumerate(values):
        result = jnp.where(index == i, F32(value), result)
    return result


def cos_turn(turn):
    angles = [2.0 * math.pi * i / PATCH for i in range(PATCH)]
    return chosen(turn & (PATCH - 1), [math.cos(a) for a in angles])


def table_shapes():
    width = GROUP * 2 * PATCH
    return (
        (2 * PATCH, 3 * PATCH),
        (2 * width, width),
        (2 * width, width),
        (width, width),
        (width, width),
        (width, 2 * width),
        (width, 2 * width),
        (PATCH, 6 * PATCH),
    )


def fill_tables(look, look_t, fwd_col, frh, frl, box, ones, irh, irl, inv_col):
    quarter = PATCH // 4
    pair = 2 * PATCH
    width = GROUP * pair
    scale = 1.0 / (AZ * RG)
    hit = ids(look.shape, 1) // RG == ids(look.shape, 0)
    look[...] = jnp.where(hit, F32(scale), F32(0.0)).astype(BF16)
    hit = ids(look_t.shape, 0) // RG == ids(look_t.shape, 1)
    look_t[...] = jnp.where(hit, F32(scale), F32(0.0)).astype(BF16)

    row, col = ids(fwd_col.shape, 0), ids(fwd_col.shape, 1)
    value = cos_turn((row & (PATCH - 1)) * (col & (PATCH - 1)) - quarter * (row >> 5))
    high = value.astype(BF16).astype(F32)
    fwd_col[...] = jnp.where(col < 2 * PATCH, high, value - high).astype(BF16)

    row, col = ids(inv_col.shape, 0), ids(inv_col.shape, 1)
    waves = [math.sin(math.pi * (u + 0.5) / PATCH) ** 2 / PATCH**2 for u in range(PATCH)]
    value = chosen(row, waves) * cos_turn(
        row * (col & (PATCH - 1)) - quarter * ((col >> 5) & 1)
    )
    high = value.astype(BF16).astype(F32)
    inv_col[...] = jnp.where(col < 2 * pair, high, value - high).astype(BF16)

    row, col = ids((pair, width), 0), ids((pair, width), 1)
    turn = (row & (PATCH - 1)) * (col & (PATCH - 1))
    lift = quarter * (((col >> 5) & 1) - (row >> 5))
    apart = (row - col) & (PATCH - 1)
    near = (apart == 0) | (apart == 1) | (apart == PATCH - 1)
    same = (row >> 5) == ((col >> 5) & 1)
    for block, turns in enumerate((turn + lift, turn + lift + quarter)):
        value = cos_turn(turns)
        for p in range(GROUP):
            high, low = split(jnp.where(col // pair == p, value, 0.0))
            frh[pl.ds(block * width + p * pair, pair)] = high
            frl[pl.ds(block * width + p * pair, pair)] = low
    for block, turns in enumerate((turn - lift, turn - lift + quarter)):
        value = cos_turn(turns)
        for p in range(GROUP):
            high, low = split(jnp.where(col // pair == p, value, 0.0))
            irh[pl.ds(p * pair, pair), pl.ds(block * width, width)] = high
            irl[pl.ds(p * pair, pair), pl.ds(block * width, width)] = low
    for p in range(GROUP):
        own = col // pair == p
        box[pl.ds(p * pair, pair)] = jnp.where(own & near, F32(1.0), F32(0.0)).astype(BF16)
        ones[pl.ds(p * pair, pair)] = jnp.where(own & same, F32(1.0), F32(0.0)).astype(BF16)


def triple(value):
    high, low = split(value)
    return jnp.concatenate([high, low, high], axis=0)


def filtered(patches, tables):
    fwd_col, frh, frl, box, ones, irh, irl, inv_col = tables
    width = frh.shape[1]
    groups = patches[0].shape[1] // width
    stacked = []
    for patch in patches:
        part = dot(fwd_col[...], triple(patch))
        for g in range(groups):
            at = slice(g * width, (g + 1) * width)
            stacked.append(jnp.concatenate([part[:PATCH, at], part[PATCH:, at]], axis=1))
    high, low = split(jnp.concatenate(stacked, axis=0))
    spec = dot(high, frh[...]) + dot(low, frh[...]) + dot(high, frl[...])
    high, low = split(spec * spec)
    rows = dot(high, box[...]) + dot(low, box[...])
    count = len(stacked)
    pieces, totals = [], []
    for k in range(count):
        r = rows[k * PATCH : (k + 1) * PATCH]
        totals.append(jnp.sum(r, axis=0, keepdims=True))
        pieces.append(r + pltpu.roll(r, 1, 0) + pltpu.roll(r, PATCH - 1, 0))
    totals += [jnp.zeros_like(totals[0])] * (-count % 8)
    high, low = split(jnp.concatenate(totals, axis=0))
    level = (dot(high, ones[...]) + dot(low, ones[...])) * (1.0 / (3 * PATCH * PATCH))
    inverse = 1.0 / (level + 1e-6)
    scaled = []
    for k in range(count):
        ratio = (pieces[k] * (1.0 / 9.0) + 0.1 * level[k : k + 1]) * inverse[k : k + 1]
        scaled.append(spec[k * PATCH : (k + 1) * PATCH] * lax.rsqrt(lax.rsqrt(ratio)))
    high, low = split(jnp.concatenate(scaled, axis=0))
    back = dot(high, irh[...]) + dot(low, irh[...]) + dot(high, irl[...])
    results = []
    for n in range(len(patches)):
        own = [back[(n * groups + g) * PATCH : (n * groups + g + 1) * PATCH] for g in range(groups)]
        real = jnp.concatenate([b[:, :width] for b in own], axis=1)
        turned = jnp.concatenate([b[:, width:] for b in own], axis=1)
        results.append(dot(inv_col[...], triple(jnp.concatenate([real, turned], axis=0))))
    return results


def gather_kernel(
    owners, tiles, pair_count, table_count, pairs_ref, slc_ref, *refs
):
    edges_ref, acc_ref, coh_ref = refs[:3]
    tables, refs = refs[3 : 3 + table_count], refs[3 + table_count :]
    chunks = slc_ref.shape[3] // LANES
    recvs, refs = refs[:chunks], refs[chunks:]
    (
        look_ref, look_t_ref, send, low_tab, slots, prods, powers, natural,
        power_looked, looked, halo_low, halo_high,
        send_sem, recv_sem, halo_send_sem, halo_recv_sem,
    ) = refs
    me = lax.axis_index("date")
    tile = lax.axis_index("tile")
    dates_here, _, rows_here, _ = slc_ref.shape
    half_rows = rows_here // AZ
    local_cols = chunks * LANES // RG
    chunk_cols = LANES // RG

    barrier = pltpu.get_barrier_semaphore()
    for offset in range(1, owners):
        pl.semaphore_signal(
            barrier, inc=1, device_id={"date": lax.rem(me + offset, owners)}, device_id_type=MESH
        )

    @pl.when(tile > 0)
    def _():
        pl.semaphore_signal(barrier, inc=1, device_id={"tile": tile - 1}, device_id_type=MESH)

    @pl.when(tile < tiles - 1)
    def _():
        pl.semaphore_signal(barrier, inc=1, device_id={"tile": tile + 1}, device_id_type=MESH)

    def ends(block, source):
        first = source * dates_here

        def step(i, carry):
            low, high = carry
            for c in range(2):
                date = pairs_ref[c, block * pair_count + i] - first
                inside = (date >= 0) & (date < dates_here)
                low = jnp.where(inside, jnp.minimum(low, date), low)
                high = jnp.where(inside, jnp.maximum(high, date), high)
            return low, high

        return lax.fori_loop(
            0, pair_count, step, (jnp.int32(dates_here - 1), jnp.int32(0)), unroll=True
        )

    def stage(target, h, low, high):
        for rank, pick in ((0, low), (1, high)):
            for part in range(2):
                target[rank, part] = slc_ref[pick, part, :, h * LANES : (h + 1) * LANES]

    def date_copy(h, offset, source, target):
        return pltpu.make_async_remote_copy(
            src_ref=send.at[h, offset - 1],
            dst_ref=recvs[h].at[source],
            send_sem=send_sem.at[h, offset - 1],
            recv_sem=recv_sem.at[h, source],
            device_id={"date": target},
            device_id_type=MESH,
        )

    below = lax.div(tile + tiles - 1, tiles)
    above = lax.div(2 * (tiles - 1) - tile, tiles)
    order = sorted(range(1, owners), key=lambda offset: abs(2 * offset - owners))
    picks = {}
    for h in range(chunks):
        for offset in order:
            target = lax.rem(me + offset, owners)
            if h == 0:
                picks[offset] = ends(target, me)
            stage(send.at[h, offset - 1], h, *picks[offset])
            if h == 0 and offset == order[0]:
                pl.semaphore_wait(barrier, owners - 1 + below + above)
            if h == 0:
                date_copy(h, offset, me, target).start()

    low, high = ends(me, me)
    for h in range(chunks):
        stage(recvs[h].at[me], h, low, high)
    for source in range(owners):
        low, _ = ends(me, jnp.int32(source))
        low_tab[source] = low + source * dates_here
    acc_ref[...] = jnp.zeros(acc_ref.shape, F32)
    fill_tables(look_ref, look_t_ref, *tables)

    def find(i, _):
        for c in range(2):
            date = pairs_ref[c, me * pair_count + i]
            source = lax.div(date, jnp.int32(dates_here))
            slots[2 * c, i] = source
            slots[2 * c + 1, i] = jnp.where(date == low_tab[source], 0, 1)
        return 0

    lax.fori_loop(0, pair_count, find, 0)

    def slot(i, c):
        return slots[2 * c, i], slots[2 * c + 1, i]

    for h in range(1, chunks):
        for offset in order:
            target = lax.rem(me + offset, owners)
            date_copy(h - 1, offset, me, target).wait_send()
            date_copy(h, offset, me, target).start()

    def halo_copy(up):
        step = 1 if up else -1
        return pltpu.make_async_remote_copy(
            src_ref=looked.at[pl.ds(local_cols - HALF if up else 0, HALF)],
            dst_ref=halo_low if up else halo_high,
            send_sem=halo_send_sem.at[0 if up else 1],
            recv_sem=halo_recv_sem.at[0 if up else 1],
            device_id={"tile": tile + step},
            device_id_type=MESH,
        )

    for h in range(chunks):
        for offset in range(1, owners):
            source = lax.rem(me + owners - offset, owners)
            date_copy(h, offset, source, source).wait_recv()

        recv = recvs[h]

        def product(i, _):
            sa, ra = slot(i, 0)
            sb, rb = slot(i, 1)
            real = jnp.zeros((half_rows, LANES), F32)
            imag = jnp.zeros((half_rows, LANES), F32)
            for odd in range(AZ):
                rows = pl.ds(odd, half_rows, stride=AZ)
                a0, a1 = recv[sa, ra, 0, rows, :], recv[sa, ra, 1, rows, :]
                b0, b1 = recv[sb, rb, 0, rows, :], recv[sb, rb, 1, rows, :]
                real = real + (a0 * b0 + a1 * b1)
                imag = imag + (a1 * b0 - a0 * b1)
            prods[i, 0] = real
            prods[i, 1] = imag
            return 0

        lax.fori_loop(0, pair_count, product, 0, unroll=4)
        high, low = split(prods[...].reshape(pair_count * 2 * half_rows, LANES))
        table = look_ref[...]
        looked[pl.ds(h * chunk_cols, chunk_cols)] = dot_nt(table, high) + dot_nt(table, low)

        if h == 0:

            @pl.when(tile > 0)
            def _():
                halo_copy(False).start()

        if h == chunks - 1:

            @pl.when(tile < tiles - 1)
            def _():
                halo_copy(True).start()

        table = look_t_ref[pl.ds(h * LANES, LANES)]
        new = (dot(high, table) + dot(low, table)).reshape(natural.shape)
        natural[...] = new if h == 0 else natural[...] + new

        def power(i, _):
            for rank in range(REQ):
                total = jnp.zeros((half_rows, LANES), F32)
                for part in range(2):
                    for odd in range(AZ):
                        field = recv[i, rank, part, pl.ds(odd, half_rows, stride=AZ), :]
                        total = total + field * field
                powers[i, rank] = total
            return 0

        lax.fori_loop(0, owners, power, 0, unroll=2)
        high, low = split(powers[...].reshape(owners * REQ * half_rows, LANES))
        new = (dot(high, table) + dot(low, table)).reshape(power_looked.shape)
        power_looked[...] = new if h == 0 else power_looked[...] + new

        per_chunk = chunk_cols // HALF
        inner = [k for k in range(h * per_chunk, (h + 1) * per_chunk) if k > 0]
        results = filtered([looked[pl.ds((k - 1) * HALF, PATCH)] for k in inner], tables)
        for k, result in zip(inner, results):
            acc_ref[pl.ds((k - 1) * HALF, PATCH)] += result

    def coherence(i, _):
        sa, ra = slot(i, 0)
        sb, rb = slot(i, 1)
        real, imag = natural[i, 0], natural[i, 1]
        coh_ref[i] = (real * real + imag * imag) / (power_looked[sa, ra] * power_looked[sb, rb])
        return 0

    lax.fori_loop(0, pair_count, coherence, 0, unroll=4)
    edges_ref[0, pl.ds(HALF, HALF)] = looked[pl.ds(0, HALF)]
    edges_ref[1, pl.ds(0, HALF)] = looked[pl.ds(local_cols - HALF, HALF)]

    @pl.when(tile > 0)
    def _():
        halo_copy(True).wait_recv()
        edges_ref[0, pl.ds(0, HALF)] = halo_low[...]

    @pl.when(tile == 0)
    def _():
        edges_ref[0, pl.ds(0, HALF)] = jnp.zeros(halo_low.shape, F32)

    @pl.when(tile < tiles - 1)
    def _():
        halo_copy(False).wait_recv()
        edges_ref[1, pl.ds(HALF, HALF)] = halo_high[...]

    @pl.when(tile == tiles - 1)
    def _():
        edges_ref[1, pl.ds(HALF, HALF)] = jnp.zeros(halo_high.shape, F32)

    @pl.when(tile < tiles - 1)
    def _():
        halo_copy(True).wait_send()

    @pl.when(tile > 0)
    def _():
        halo_copy(False).wait_send()

    for offset in range(1, owners):
        date_copy(chunks - 1, offset, me, lax.rem(me + offset, owners)).wait_send()


def filter_kernel(edges_ref, acc_ref, coh_in, *refs):
    tables, (out_ref, coh_out) = refs[:-2], refs[-2:]
    coh_out[...] = coh_in[...]
    first, last = filtered([edges_ref[0], edges_ref[1]], tables)
    final = jnp.concatenate(
        [
            acc_ref[:HALF] + first[HALF:],
            acc_ref[HALF:-HALF],
            acc_ref[-HALF:] + last[:HALF],
        ],
        axis=0,
    ).T
    for p in range(out_ref.shape[1]):
        for c in range(2):
            at = (p * 2 + c) * PATCH
            out_ref[c, p] = final[at : at + PATCH]


def local(slc, pairs):
    owners = lax.axis_size("date")
    tiles = lax.axis_size("tile")
    rows, cols = slc.shape[2], slc.shape[3]
    looked_cols = cols // RG
    half_rows = rows // AZ
    chunks = cols // LANES
    pair_count = pairs.shape[0] // owners
    lanes = pair_count * 2 * half_rows
    vmem = pl.BlockSpec(memory_space=pltpu.VMEM)
    smem = pl.BlockSpec(memory_space=pltpu.SMEM)
    tables = [jax.ShapeDtypeStruct(shape, BF16) for shape in table_shapes()]
    outs = pl.pallas_call(
        functools.partial(gather_kernel, owners, tiles, pair_count, len(tables)),
        out_shape=(
            jax.ShapeDtypeStruct((2, PATCH, lanes), F32),
            jax.ShapeDtypeStruct((looked_cols, lanes), F32),
            jax.ShapeDtypeStruct((pair_count, half_rows, looked_cols), F32),
            *tables,
        ),
        in_specs=[smem, vmem],
        out_specs=(vmem,) * (3 + len(tables)),
        scratch_shapes=[
            *[pltpu.VMEM((owners, REQ, 2, rows, LANES), F32)] * chunks,
            pltpu.VMEM((LANES // RG, LANES), BF16),
            pltpu.VMEM((cols, looked_cols), BF16),
            pltpu.VMEM((chunks, owners - 1, REQ, 2, rows, LANES), F32),
            pltpu.SMEM((owners,), jnp.int32),
            pltpu.SMEM((4, pair_count), jnp.int32),
            pltpu.VMEM((pair_count, 2, half_rows, LANES), F32),
            pltpu.VMEM((owners, REQ, half_rows, LANES), F32),
            pltpu.VMEM((pair_count, 2, half_rows, looked_cols), F32),
            pltpu.VMEM((owners, REQ, half_rows, looked_cols), F32),
            pltpu.VMEM((looked_cols, lanes), F32),
            pltpu.VMEM((HALF, lanes), F32),
            pltpu.VMEM((HALF, lanes), F32),
            pltpu.SemaphoreType.DMA((chunks, owners - 1)),
            pltpu.SemaphoreType.DMA((chunks, owners)),
            pltpu.SemaphoreType.DMA((2,)),
            pltpu.SemaphoreType.DMA((2,)),
        ],
        compiler_params=pltpu.CompilerParams(
            collective_id=0, has_side_effects=True, vmem_limit_bytes=40 * 2**20
        ),
        name="gather_looks",
    )(pairs.T, slc)
    return pl.pallas_call(
        filter_kernel,
        out_shape=(
            jax.ShapeDtypeStruct((2, pair_count, half_rows, looked_cols), F32),
            jax.ShapeDtypeStruct((pair_count, half_rows, looked_cols), F32),
        ),
        in_specs=[vmem] * len(outs),
        out_specs=(vmem, vmem),
        compiler_params=pltpu.CompilerParams(vmem_limit_bytes=40 * 2**20),
        name="filter_edges",
    )(*outs)


def solution(mesh):
    placed = (P("date", None, "groups", "tile"), P())
    return jax.shard_map(
        local,
        mesh=mesh,
        in_specs=placed,
        out_specs=(P(None, "date", "groups", "tile"), P("date", "groups", "tile")),
        check_vma=False,
    )
```

```python
import functools
import math

import jax
import jax.numpy as jnp
from jax import lax
from jax.experimental import pallas as pl
from jax.experimental.pallas import tpu as pltpu
from jax.sharding import PartitionSpec as P

REQ = 2
AZ = 2
RG = 4
PATCH = 32
HALF = PATCH // 2
GROUP = 4
LANES = 128
MESH = pl.DeviceIdType.MESH
F32 = jnp.float32
BF16 = jnp.bfloat16


def split(value):
    high = value.astype(BF16)
    low = (value - high.astype(F32)).astype(BF16)
    return high, low


def dot(a, b):
    return jnp.dot(a, b, preferred_element_type=F32)


def dot_nt(a, b):
    return lax.dot_general(a, b, (((1,), (1,)), ((), ())), preferred_element_type=F32)


def ids(shape, axis):
    return lax.broadcasted_iota(jnp.int32, shape, axis)


def chosen(index, values):
    result = jnp.zeros(index.shape, F32)
    for i, value in enumerate(values):
        result = jnp.where(index == i, F32(value), result)
    return result


def cos_turn(turn):
    angles = [2.0 * math.pi * i / PATCH for i in range(PATCH)]
    return chosen(turn & (PATCH - 1), [math.cos(a) for a in angles])


def table_shapes():
    width = GROUP * 2 * PATCH
    return (
        (2 * PATCH, 3 * PATCH),
        (2 * width, width),
        (2 * width, width),
        (width, width),
        (width, width),
        (width, 2 * width),
        (width, 2 * width),
        (PATCH, 6 * PATCH),
    )


def fill_tables(look, look_t, fwd_col, frh, frl, box, ones, irh, irl, inv_col):
    quarter = PATCH // 4
    pair = 2 * PATCH
    width = GROUP * pair
    scale = 1.0 / (AZ * RG)
    hit = ids(look.shape, 1) // RG == ids(look.shape, 0)
    look[...] = jnp.where(hit, F32(scale), F32(0.0)).astype(BF16)
    hit = ids(look_t.shape, 0) // RG == ids(look_t.shape, 1)
    look_t[...] = jnp.where(hit, F32(scale), F32(0.0)).astype(BF16)

    row, col = ids(fwd_col.shape, 0), ids(fwd_col.shape, 1)
    value = cos_turn((row & (PATCH - 1)) * (col & (PATCH - 1)) - quarter * (row >> 5))
    high = value.astype(BF16).astype(F32)
    fwd_col[...] = jnp.where(col < 2 * PATCH, high, value - high).astype(BF16)

    row, col = ids(inv_col.shape, 0), ids(inv_col.shape, 1)
    waves = [math.sin(math.pi * (u + 0.5) / PATCH) ** 2 / PATCH**2 for u in range(PATCH)]
    value = chosen(row, waves) * cos_turn(
        row * (col & (PATCH - 1)) - quarter * ((col >> 5) & 1)
    )
    high = value.astype(BF16).astype(F32)
    inv_col[...] = jnp.where(col < 2 * pair, high, value - high).astype(BF16)

    row, col = ids((pair, width), 0), ids((pair, width), 1)
    turn = (row & (PATCH - 1)) * (col & (PATCH - 1))
    lift = quarter * (((col >> 5) & 1) - (row >> 5))
    apart = (row - col) & (PATCH - 1)
    near = (apart == 0) | (apart == 1) | (apart == PATCH - 1)
    same = (row >> 5) == ((col >> 5) & 1)
    for block, turns in enumerate((turn + lift, turn + lift + quarter)):
        value = cos_turn(turns)
        for p in range(GROUP):
            high, low = split(jnp.where(col // pair == p, value, 0.0))
            frh[pl.ds(block * width + p * pair, pair)] = high
            frl[pl.ds(block * width + p * pair, pair)] = low
    for block, turns in enumerate((turn - lift, turn - lift + quarter)):
        value = cos_turn(turns)
        for p in range(GROUP):
            high, low = split(jnp.where(col // pair == p, value, 0.0))
            irh[pl.ds(p * pair, pair), pl.ds(block * width, width)] = high
            irl[pl.ds(p * pair, pair), pl.ds(block * width, width)] = low
    for p in range(GROUP):
        own = col // pair == p
        box[pl.ds(p * pair, pair)] = jnp.where(own & near, F32(1.0), F32(0.0)).astype(BF16)
        ones[pl.ds(p * pair, pair)] = jnp.where(own & same, F32(1.0), F32(0.0)).astype(BF16)


def triple(value):
    high, low = split(value)
    return jnp.concatenate([high, low, high], axis=0)


def filtered(patches, tables):
    fwd_col, frh, frl, box, ones, irh, irl, inv_col = tables
    width = frh.shape[1]
    groups = patches[0].shape[1] // width
    stacked = []
    for patch in patches:
        part = dot(fwd_col[...], triple(patch))
        for g in range(groups):
            at = slice(g * width, (g + 1) * width)
            stacked.append(jnp.concatenate([part[:PATCH, at], part[PATCH:, at]], axis=1))
    high, low = split(jnp.concatenate(stacked, axis=0))
    spec = dot(high, frh[...]) + dot(low, frh[...]) + dot(high, frl[...])
    high, low = split(spec * spec)
    rows = dot(high, box[...]) + dot(low, box[...])
    count = len(stacked)
    pieces, totals = [], []
    for k in range(count):
        r = rows[k * PATCH : (k + 1) * PATCH]
        totals.append(jnp.sum(r, axis=0, keepdims=True))
        pieces.append(r + pltpu.roll(r, 1, 0) + pltpu.roll(r, PATCH - 1, 0))
    totals += [jnp.zeros_like(totals[0])] * (-count % 8)
    high, low = split(jnp.concatenate(totals, axis=0))
    level = (dot(high, ones[...]) + dot(low, ones[...])) * (1.0 / (3 * PATCH * PATCH))
    inverse = 1.0 / (level + 1e-6)
    scaled = []
    for k in range(count):
        ratio = (pieces[k] * (1.0 / 9.0) + 0.1 * level[k : k + 1]) * inverse[k : k + 1]
        scaled.append(spec[k * PATCH : (k + 1) * PATCH] * lax.rsqrt(lax.rsqrt(ratio)))
    high, low = split(jnp.concatenate(scaled, axis=0))
    back = dot(high, irh[...]) + dot(low, irh[...]) + dot(high, irl[...])
    results = []
    for n in range(len(patches)):
        own = [back[(n * groups + g) * PATCH : (n * groups + g + 1) * PATCH] for g in range(groups)]
        real = jnp.concatenate([b[:, :width] for b in own], axis=1)
        turned = jnp.concatenate([b[:, width:] for b in own], axis=1)
        results.append(dot(inv_col[...], triple(jnp.concatenate([real, turned], axis=0))))
    return results


def gather_kernel(
    owners, tiles, pair_count, table_count, pairs_ref, slc_ref, *refs
):
    edges_ref, acc_ref, coh_ref = refs[:3]
    tables, refs = refs[3 : 3 + table_count], refs[3 + table_count :]
    chunks = slc_ref.shape[3] // LANES
    recvs, refs = refs[:chunks], refs[chunks:]
    (
        look_ref, look_t_ref, send, low_tab, slots, prods, powers, natural,
        power_looked, looked, halo_low, halo_high,
        send_sem, recv_sem, halo_send_sem, halo_recv_sem,
    ) = refs
    me = lax.axis_index("date")
    tile = lax.axis_index("tile")
    dates_here, _, rows_here, _ = slc_ref.shape
    half_rows = rows_here // AZ
    local_cols = chunks * LANES // RG
    chunk_cols = LANES // RG

    barrier = pltpu.get_barrier_semaphore()
    for offset in range(1, owners):
        pl.semaphore_signal(
            barrier, inc=1, device_id={"date": lax.rem(me + offset, owners)}, device_id_type=MESH
        )

    @pl.when(tile > 0)
    def _():
        pl.semaphore_signal(barrier, inc=1, device_id={"tile": tile - 1}, device_id_type=MESH)

    @pl.when(tile < tiles - 1)
    def _():
        pl.semaphore_signal(barrier, inc=1, device_id={"tile": tile + 1}, device_id_type=MESH)

    def ends(block, source):
        first = source * dates_here

        def step(i, carry):
            low, high = carry
            for c in range(2):
                date = pairs_ref[c, block * pair_count + i] - first
                inside = (date >= 0) & (date < dates_here)
                low = jnp.where(inside, jnp.minimum(low, date), low)
                high = jnp.where(inside, jnp.maximum(high, date), high)
            return low, high

        return lax.fori_loop(
            0, pair_count, step, (jnp.int32(dates_here - 1), jnp.int32(0)), unroll=True
        )

    def stage(target, h, low, high):
        for rank, pick in ((0, low), (1, high)):
            for part in range(2):
                target[rank, part] = slc_ref[pick, part, :, h * LANES : (h + 1) * LANES]

    def date_copy(h, offset, source, target):
        return pltpu.make_async_remote_copy(
            src_ref=send.at[h, offset - 1],
            dst_ref=recvs[h].at[source],
            send_sem=send_sem.at[h, offset - 1],
            recv_sem=recv_sem.at[h, source],
            device_id={"date": target},
            device_id_type=MESH,
        )

    below = lax.div(tile + tiles - 1, tiles)
    above = lax.div(2 * (tiles - 1) - tile, tiles)
    order = sorted(range(1, owners), key=lambda offset: abs(2 * offset - owners))
    picks = {}
    for h in range(chunks):
        for offset in order:
            target = lax.rem(me + offset, owners)
            if h == 0:
                picks[offset] = ends(target, me)
            stage(send.at[h, offset - 1], h, *picks[offset])
            if h == 0 and offset == order[0]:
                pl.semaphore_wait(barrier, owners - 1 + below + above)
            date_copy(h, offset, me, target).start()

    low, high = ends(me, me)
    for h in range(chunks):
        stage(recvs[h].at[me], h, low, high)
    for source in range(owners):
        low, _ = ends(me, jnp.int32(source))
        low_tab[source] = low + source * dates_here
    acc_ref[...] = jnp.zeros(acc_ref.shape, F32)
    fill_tables(look_ref, look_t_ref, *tables)

    def find(i, _):
        for c in range(2):
            date = pairs_ref[c, me * pair_count + i]
            source = lax.div(date, jnp.int32(dates_here))
            slots[2 * c, i] = source
            slots[2 * c + 1, i] = jnp.where(date == low_tab[source], 0, 1)
        return 0

    lax.fori_loop(0, pair_count, find, 0)

    def slot(i, c):
        return slots[2 * c, i], slots[2 * c + 1, i]

    def halo_copy(up):
        step = 1 if up else -1
        return pltpu.make_async_remote_copy(
            src_ref=looked.at[pl.ds(local_cols - HALF if up else 0, HALF)],
            dst_ref=halo_low if up else halo_high,
            send_sem=halo_send_sem.at[0 if up else 1],
            recv_sem=halo_recv_sem.at[0 if up else 1],
            device_id={"tile": tile + step},
            device_id_type=MESH,
        )

    for h in range(chunks):
        for offset in range(1, owners):
            source = lax.rem(me + owners - offset, owners)
            date_copy(h, offset, source, source).wait_recv()

        recv = recvs[h]

        def product(i, _):
            sa, ra = slot(i, 0)
            sb, rb = slot(i, 1)
            real = jnp.zeros((half_rows, LANES), F32)
            imag = jnp.zeros((half_rows, LANES), F32)
            for odd in range(AZ):
                rows = pl.ds(odd, half_rows, stride=AZ)
                a0, a1 = recv[sa, ra, 0, rows, :], recv[sa, ra, 1, rows, :]
                b0, b1 = recv[sb, rb, 0, rows, :], recv[sb, rb, 1, rows, :]
                real = real + (a0 * b0 + a1 * b1)
                imag = imag + (a1 * b0 - a0 * b1)
            prods[i, 0] = real
            prods[i, 1] = imag
            return 0

        lax.fori_loop(0, pair_count, product, 0, unroll=4)
        high, low = split(prods[...].reshape(pair_count * 2 * half_rows, LANES))
        table = look_ref[...]
        looked[pl.ds(h * chunk_cols, chunk_cols)] = dot_nt(table, high) + dot_nt(table, low)

        if h == 0:

            @pl.when(tile > 0)
            def _():
                halo_copy(False).start()

        if h == chunks - 1:

            @pl.when(tile < tiles - 1)
            def _():
                halo_copy(True).start()

        table = look_t_ref[pl.ds(h * LANES, LANES)]
        new = (dot(high, table) + dot(low, table)).reshape(natural.shape)
        natural[...] = new if h == 0 else natural[...] + new

        def power(i, _):
            for rank in range(REQ):
                total = jnp.zeros((half_rows, LANES), F32)
                for part in range(2):
                    for odd in range(AZ):
                        field = recv[i, rank, part, pl.ds(odd, half_rows, stride=AZ), :]
                        total = total + field * field
                powers[i, rank] = total
            return 0

        lax.fori_loop(0, owners, power, 0, unroll=2)
        high, low = split(powers[...].reshape(owners * REQ * half_rows, LANES))
        new = (dot(high, table) + dot(low, table)).reshape(power_looked.shape)
        power_looked[...] = new if h == 0 else power_looked[...] + new

        per_chunk = chunk_cols // HALF
        inner = [k for k in range(h * per_chunk, (h + 1) * per_chunk) if k > 0]
        if h == chunks - 1:
            for n, k in enumerate(inner):
                edges_ref[2 + n] = looked[pl.ds((k - 1) * HALF, PATCH)]
            continue
        results = filtered([looked[pl.ds((k - 1) * HALF, PATCH)] for k in inner], tables)
        for k, result in zip(inner, results):
            acc_ref[pl.ds((k - 1) * HALF, PATCH)] += result

    def coherence(i, _):
        sa, ra = slot(i, 0)
        sb, rb = slot(i, 1)
        real, imag = natural[i, 0], natural[i, 1]
        coh_ref[i] = (real * real + imag * imag) / (power_looked[sa, ra] * power_looked[sb, rb])
        return 0

    lax.fori_loop(0, pair_count, coherence, 0, unroll=4)
    edges_ref[0, pl.ds(HALF, HALF)] = looked[pl.ds(0, HALF)]
    edges_ref[1, pl.ds(0, HALF)] = looked[pl.ds(local_cols - HALF, HALF)]

    @pl.when(tile > 0)
    def _():
        halo_copy(True).wait_recv()
        edges_ref[0, pl.ds(0, HALF)] = halo_low[...]

    @pl.when(tile == 0)
    def _():
        edges_ref[0, pl.ds(0, HALF)] = jnp.zeros(halo_low.shape, F32)

    @pl.when(tile < tiles - 1)
    def _():
        halo_copy(False).wait_recv()
        edges_ref[1, pl.ds(HALF, HALF)] = halo_high[...]

    @pl.when(tile == tiles - 1)
    def _():
        edges_ref[1, pl.ds(HALF, HALF)] = jnp.zeros(halo_high.shape, F32)

    @pl.when(tile < tiles - 1)
    def _():
        halo_copy(True).wait_send()

    @pl.when(tile > 0)
    def _():
        halo_copy(False).wait_send()

    for h in range(chunks):
        for offset in range(1, owners):
            date_copy(h, offset, me, lax.rem(me + offset, owners)).wait_send()


def filter_kernel(edges_ref, acc_ref, coh_in, *refs):
    tables, (out_ref, coh_out) = refs[:-2], refs[-2:]
    coh_out[...] = coh_in[...]
    count = acc_ref.shape[0] // HALF
    sums = [acc_ref[b * HALF : (b + 1) * HALF] for b in range(count)]
    fields = [edges_ref[n] for n in range(edges_ref.shape[0])]
    late = len(fields) - 2
    for k, result in zip((0, count, *range(count - late, count)), filtered(fields, tables)):
        if k > 0:
            sums[k - 1] = sums[k - 1] + result[:HALF]
        if k < count:
            sums[k] = sums[k] + result[HALF:]
    final = jnp.concatenate(sums, axis=0).T
    for p in range(out_ref.shape[1]):
        for c in range(2):
            at = (p * 2 + c) * PATCH
            out_ref[c, p] = final[at : at + PATCH]


def local(slc, pairs):
    owners = lax.axis_size("date")
    tiles = lax.axis_size("tile")
    rows, cols = slc.shape[2], slc.shape[3]
    looked_cols = cols // RG
    half_rows = rows // AZ
    chunks = cols // LANES
    pair_count = pairs.shape[0] // owners
    lanes = pair_count * 2 * half_rows
    late = LANES // RG // HALF - (chunks == 1)
    vmem = pl.BlockSpec(memory_space=pltpu.VMEM)
    smem = pl.BlockSpec(memory_space=pltpu.SMEM)
    tables = [jax.ShapeDtypeStruct(shape, BF16) for shape in table_shapes()]
    outs = pl.pallas_call(
        functools.partial(gather_kernel, owners, tiles, pair_count, len(tables)),
        out_shape=(
            jax.ShapeDtypeStruct((2 + late, PATCH, lanes), F32),
            jax.ShapeDtypeStruct((looked_cols, lanes), F32),
            jax.ShapeDtypeStruct((pair_count, half_rows, looked_cols), F32),
            *tables,
        ),
        in_specs=[smem, vmem],
        out_specs=(vmem,) * (3 + len(tables)),
        scratch_shapes=[
            *[pltpu.VMEM((owners, REQ, 2, rows, LANES), F32)] * chunks,
            pltpu.VMEM((LANES // RG, LANES), BF16),
            pltpu.VMEM((cols, looked_cols), BF16),
            pltpu.VMEM((chunks, owners - 1, REQ, 2, rows, LANES), F32),
            pltpu.SMEM((owners,), jnp.int32),
            pltpu.SMEM((4, pair_count), jnp.int32),
            pltpu.VMEM((pair_count, 2, half_rows, LANES), F32),
            pltpu.VMEM((owners, REQ, half_rows, LANES), F32),
            pltpu.VMEM((pair_count, 2, half_rows, looked_cols), F32),
            pltpu.VMEM((owners, REQ, half_rows, looked_cols), F32),
            pltpu.VMEM((looked_cols, lanes), F32),
            pltpu.VMEM((HALF, lanes), F32),
            pltpu.VMEM((HALF, lanes), F32),
            pltpu.SemaphoreType.DMA((chunks, owners - 1)),
            pltpu.SemaphoreType.DMA((chunks, owners)),
            pltpu.SemaphoreType.DMA((2,)),
            pltpu.SemaphoreType.DMA((2,)),
        ],
        compiler_params=pltpu.CompilerParams(
            collective_id=0, has_side_effects=True, vmem_limit_bytes=40 * 2**20
        ),
        name="gather_looks",
    )(pairs.T, slc)
    return pl.pallas_call(
        filter_kernel,
        out_shape=(
            jax.ShapeDtypeStruct((2, pair_count, half_rows, looked_cols), F32),
            jax.ShapeDtypeStruct((pair_count, half_rows, looked_cols), F32),
        ),
        in_specs=[vmem] * len(outs),
        out_specs=(vmem, vmem),
        compiler_params=pltpu.CompilerParams(vmem_limit_bytes=40 * 2**20),
        name="filter_edges",
    )(*outs)


def solution(mesh):
    placed = (P("date", None, "groups", "tile"), P())
    return jax.shard_map(
        local,
        mesh=mesh,
        in_specs=placed,
        out_specs=(P(None, "date", "groups", "tile"), P("date", "groups", "tile")),
        check_vma=False,
    )
```
